256 devices in a mesh: node: 16 (over x, y), local: 8 (over z), replica: 2 (over core).
Axes of the slice: x: 4, y: 4, z: 8, core: 2. Of those that a mesh axis runs over, the one named last changes fastest.
Arguments:
- out_grad: bfloat16 [32768, 3584], P(('node', 'local', 'replica')), may hold values from -6 to 6
- expert_ids: int32 [32768, 8], P(('node', 'local', 'replica')), may hold values from 0 to 127, as said below
- drop_flags: int32 [32768, 8], P(('node', 'local', 'replica')), may hold values from 0 to 1, as said below
- router_logits: float32 [32768, 8], P(('node', 'local', 'replica')), may hold values from -4 to 4
- saved_hidden: bfloat16 [2, 128, 768, 1024], P('replica', ('node', 'local')), may hold values from -1.1953125 to 1.1953125
- down_weight: bfloat16 [128, 3584, 1024], P(('node', 'local'), 'replica'), may hold values from -0.09375 to 0.09375
Outputs:
- grad_logits: float32 [32768, 8], P(('node', 'local', 'replica'))
- grad_hidden: bfloat16 [2, 128, 768, 1024], P('replica', ('node', 'local'))
- grad_down: bfloat16 [128, 3584, 1024], P(('node', 'local'), 'replica')
The draws below stay inside these ranges and needn't reach their ends.
Inputs may be any that keep to these rules, and one draw needn't show every extreme that they name: `expert_ids`: each row names 8 different experts, all from at most 4 groups of 8 consecutive experts. `drop_flags`: among the kept pairs of one device's 128 rows, at most 6 name the same expert; in every draw some expert gets exactly 6 kept pairs from every device's rows.
All inputs are finite; a program needn't handle non-finite values.
Results may differ from the reference program's by a relative error of at most 0.0057.
Values may be sent and summed in bfloat16 or wider, within the bound.
No kernel may reach another device: no remote copies, remote signals or barrier semaphores. Data moves between devices by JAX's collectives and lax.ppermute only.
A program may use at most 128 MiB of HBM per device.

```python
import jax
import jax.numpy as jnp
from jax import lax

D = 3584
F = 1024
TOPK = 8
TOK_DEV = 128
EXPERT_GROUPS = 16
GROUP_EXPERTS = 8
ROUTED_EXPERTS = 128
PICKED = 4
REPLICAS = 2
CAP_PAIR = 6
SLOTS = 768
TOTAL_TOKENS = 32768


def routing_draw(key):
    key = jax.random.fold_in(key, 101)
    random_keys = jax.random.split(key, 5)
    hot_expert = jax.random.randint(random_keys[0], (), 0, ROUTED_EXPERTS)
    group_offset_bias = jax.random.randint(random_keys[1], (EXPERT_GROUPS,), 0, 1 << 15)
    expert_offset_bias = jax.random.randint(random_keys[2], (ROUTED_EXPERTS,), 0, 1 << 15)
    row_index = jnp.arange(TOTAL_TOKENS, dtype=jnp.int32)
    forced = row_index % TOK_DEV < CAP_PAIR
    group_row = jnp.arange(EXPERT_GROUPS, dtype=jnp.int32)
    expert_row = jnp.arange(ROUTED_EXPERTS, dtype=jnp.int32)
    group_affinity_score = jax.random.randint(random_keys[3], (TOTAL_TOKENS, EXPERT_GROUPS), 0, 1 << 16) + group_offset_bias[None, :]
    hot_group = forced[:, None] & (group_row[None, :] == hot_expert // GROUP_EXPERTS)
    group_affinity_score = group_affinity_score + jnp.where(hot_group, 1 << 18, 0)
    group_affinity_score = group_affinity_score * EXPERT_GROUPS + group_row[None, :]
    unused, chosen = lax.top_k(group_affinity_score, PICKED)
    allowed = jnp.any(chosen[:, :, None] == (expert_row // GROUP_EXPERTS)[None, None, :], axis=1)
    expert_affinity_score = jax.random.randint(random_keys[4], (TOTAL_TOKENS, ROUTED_EXPERTS), 0, 1 << 16) + expert_offset_bias[None, :] + 1
    hot_column = forced[:, None] & (expert_row[None, :] == hot_expert)
    expert_affinity_score = expert_affinity_score + jnp.where(hot_column, 1 << 18, 0)
    expert_affinity_score = jnp.where(allowed, expert_affinity_score, 0) * ROUTED_EXPERTS + expert_row[None, :]
    unused, picked = lax.top_k(expert_affinity_score, TOPK)
    return (picked.astype(jnp.int32), hot_expert, forced)


def draw_expert_ids(key, part):
    picked, hot_expert, forced = routing_draw(key)
    return picked


def draw_drop_flags(key, part):
    picked, hot_expert, forced = routing_draw(key)
    key = jax.random.fold_in(key, 202)
    random_drop = jax.random.randint(key, (TOTAL_TOKENS, TOPK), 0, 8) == 0
    protected = forced[:, None] & (picked == hot_expert)
    random_drop = random_drop & jnp.logical_not(protected)
    kept_pair = jnp.where(random_drop, 0, 1).astype(jnp.int32)
    blocks = TOTAL_TOKENS // TOK_DEV
    expert_row = jnp.arange(ROUTED_EXPERTS, dtype=jnp.int32)

    def block_rank(block_item):
        ids_block, kept_block = block_item
        onehot = (ids_block[:, None] == expert_row[None, :]).astype(jnp.int32) * kept_block[:, None]
        before = jnp.cumsum(onehot, axis=0) - onehot
        return jnp.sum(before * onehot, axis=1)
    pair_rank = lax.map(block_rank, (picked.reshape(blocks, TOK_DEV * TOPK), kept_pair.reshape(blocks, TOK_DEV * TOPK)))
    pair_rank = pair_rank.reshape(TOTAL_TOKENS, TOPK)
    over_cap = (kept_pair > 0) & (pair_rank >= CAP_PAIR)
    return jnp.where(random_drop | over_cap, 1, 0).astype(jnp.int32)


def steps_of(rng, shape, cuts, least, largest):
    loudness, own = 1.0, jax.random.fold_in(rng, 6)
    for dim, parts in cuts:
        heights = jnp.exp(jax.random.uniform(jax.random.fold_in(own, dim), (parts,), jnp.float32, least / len(cuts), largest / len(cuts)))
        loudness = loudness * jnp.repeat(heights, shape[dim] // parts).reshape([-1 if axis == dim else 1 for axis in range(len(shape))])
    return loudness


def centred(stream_key, extent, scale, limit, pieces=(), kind=jnp.bfloat16):
    loudness = steps_of(stream_key, extent, pieces, -0.22, 0.18) if pieces else 1.0
    values = jax.random.normal(stream_key, extent, jnp.float32) * scale * loudness
    return jnp.minimum(jnp.maximum(values, -limit), limit).astype(kind)


def setup_inputs(seed: int = 0) -> dict:
    seeds = jax.random.split(jax.random.key(seed), 7)
    return {
        "out_grad": centred(seeds[0], (TOTAL_TOKENS, D), 1.0, 6.0, ((0, 256),)),
        "expert_ids": draw_expert_ids(jax.random.fold_in(seeds[6], 71), 0),
        "drop_flags": draw_drop_flags(jax.random.fold_in(seeds[6], 71), 0),
        "router_logits": centred(seeds[3], (TOTAL_TOKENS, TOPK), 1.0, 4.0, ((0, 256),), jnp.float32),
        "saved_hidden": centred(seeds[4], (REPLICAS, ROUTED_EXPERTS, SLOTS, F), 0.2, 1.1953125, ((0, 2), (1, 128))),
        "down_weight": centred(seeds[5], (ROUTED_EXPERTS, D, F), D ** -0.5, 0.09375, ((0, 128), (1, 2))),
    }


route_scale = 2.5


def reference(out_grad, expert_ids, drop_flags, router_logits, saved_hidden, down_weight):
    blocks = TOTAL_TOKENS // TOK_DEV
    per_block = TOK_DEV * TOPK
    kept_pair = (1 - drop_flags).astype(jnp.int32).reshape(blocks, per_block)
    pair_ids = expert_ids.astype(jnp.int32).reshape(blocks, per_block)
    expert_row = jnp.arange(ROUTED_EXPERTS, dtype=jnp.int32)

    def block_rank(block_item):
        ids_block, kept_block = block_item
        onehot = (ids_block[:, None] == expert_row[None, :]).astype(jnp.int32) * kept_block[:, None]
        before = jnp.cumsum(onehot, axis=0) - onehot
        return jnp.sum(before * onehot, axis=1).astype(jnp.int32)

    pair_rank = lax.map(block_rank, (pair_ids, kept_pair))
    block_index = jnp.arange(blocks, dtype=jnp.int32)[:, None]
    replica_of = block_index % REPLICAS
    source_of = block_index // REPLICAS
    slot_count = REPLICAS * ROUTED_EXPERTS * SLOTS
    target = (replica_of * ROUTED_EXPERTS + pair_ids) * SLOTS + source_of * CAP_PAIR + pair_rank
    target = jnp.where(kept_pair > 0, target, slot_count).reshape(-1).astype(jnp.int32)
    pair_index = jnp.arange(blocks * per_block, dtype=jnp.int32)
    pair_of_slot = jnp.full((slot_count,), -1, jnp.int32).at[target].set(pair_index, mode="drop")

    affinity = jax.nn.sigmoid(router_logits.astype(jnp.float32))
    denominator = jnp.sum(affinity, axis=1, keepdims=True)
    gate_sent = (route_scale * affinity / denominator).astype(jnp.bfloat16).reshape(-1)

    def expert_step(expert):
        weight = lax.dynamic_index_in_dim(down_weight, expert, 0, keepdims=False)
        summed = jnp.zeros((D, F), jnp.float32)
        grad_list = []
        gate_list = []
        for replica in range(REPLICAS):
            slot_index = lax.dynamic_slice_in_dim(pair_of_slot, (replica * ROUTED_EXPERTS + expert) * SLOTS, SLOTS)
            live_slot = slot_index >= 0
            safe_index = jnp.maximum(slot_index, 0).astype(jnp.int32)
            slot_rows = jnp.where(live_slot[:, None], out_grad[safe_index // TOPK], jnp.zeros((), jnp.bfloat16))
            slot_gate = jnp.where(live_slot, gate_sent[safe_index].astype(jnp.float32), jnp.float32(0.0))
            hidden = lax.dynamic_index_in_dim(saved_hidden[replica], expert, 0, keepdims=False)
            backward = jnp.dot(slot_rows, weight, preferred_element_type=jnp.float32)
            grad_list.append((slot_gate[:, None] * backward).astype(jnp.bfloat16))
            gate_list.append(jnp.sum(hidden.astype(jnp.float32) * backward, axis=1))
            scaled = (slot_gate[:, None] * slot_rows.astype(jnp.float32)).astype(jnp.bfloat16)
            summed = summed + jnp.dot(scaled.T, hidden, preferred_element_type=jnp.float32)
        return jnp.stack(grad_list), jnp.stack(gate_list), summed.astype(jnp.bfloat16)

    grad_rows, gate_rows, grad_down = lax.map(expert_step, jnp.arange(ROUTED_EXPERTS, dtype=jnp.int32))
    grad_hidden = jnp.transpose(grad_rows, (1, 0, 2, 3))
    gate_flat = jnp.transpose(gate_rows, (1, 0, 2)).reshape(-1)
    clipped = jnp.minimum(target, slot_count - 1).astype(jnp.int32)
    pair_grad = jnp.where(target < slot_count, gate_flat[clipped], jnp.float32(0.0)).reshape(TOTAL_TOKENS, TOPK)
    weighted = jnp.sum(pair_grad * affinity, axis=1, keepdims=True)
    grad_affinity = route_scale * (pair_grad / denominator - weighted / (denominator * denominator))
    grad_logits = (grad_affinity * affinity * (1.0 - affinity)).astype(jnp.float32)
    return grad_logits, grad_hidden, grad_down
```

```python
import functools

import jax
import jax.numpy as jnp
from jax import lax
from jax.experimental import pallas as pl
from jax.experimental.pallas import tpu as pltpu
from jax.sharding import PartitionSpec as P

route_scale = 2.5
bf16 = jnp.bfloat16
f32 = jnp.float32
EARLY = 1280
NODES = 16
RING = 8
CAP = 6
TOPK = 8
BLOCK = RING * CAP
LANES = 128
SLOTS = NODES * BLOCK
RING_SPLIT = 1152
VMEM_LIMIT = 14 * 2**20


def route_kernel(z_ref, *refs):
    infos, (select_ref, gate_ref) = refs[:RING], refs[RING:]
    slots = SLOTS
    z = z_ref[0]
    expert = (lax.broadcasted_iota(jnp.int32, (NODES, LANES), 0) * RING + z).astype(f32)
    before = (
        lax.broadcasted_iota(jnp.int32, (LANES, LANES), 0)
        < lax.broadcasted_iota(jnp.int32, (LANES, LANES), 1)
    ).astype(bf16)
    spread = (
        lax.broadcasted_iota(jnp.int32, (slots, NODES), 0) // BLOCK
        == lax.broadcasted_iota(jnp.int32, (slots, NODES), 1)
    ).astype(bf16)
    row = lax.broadcasted_iota(jnp.int32, (slots, LANES), 0) % BLOCK
    source = row // CAP
    wanted = (row % CAP + 1).astype(f32)
    slot_gate = jnp.zeros((slots, LANES), f32)
    for j in range(RING):
        info = infos[j][...].astype(f32).T
        code, gate = info[:TOPK], info[TOPK : 2 * TOPK]
        match = jnp.zeros((NODES, LANES), f32)
        match_gate = jnp.zeros((NODES, LANES), f32)
        for k in range(TOPK):
            hit = expert == code[k : k + 1]
            match = match + jnp.where(hit, 1.0, 0.0)
            match_gate = match_gate + jnp.where(hit, gate[k : k + 1], 0.0)
        rank = jnp.dot(match.astype(bf16), before, preferred_element_type=f32)
        order = (match * (rank + 1.0)).astype(bf16)
        order = jnp.dot(spread, order, preferred_element_type=f32)
        spread_gate = jnp.dot(spread, match_gate.astype(bf16), preferred_element_type=f32)
        origin = lax.rem(z + RING - j, RING)
        here = (order == wanted) & (source == origin)
        block = jnp.where(here, 1.0, 0.0).astype(bf16)
        select_ref[:, j * LANES : (j + 1) * LANES] = block
        slot_gate = slot_gate + jnp.where(here, spread_gate, 0.0)
    total = jnp.sum(slot_gate, axis=1, keepdims=True)
    gate_ref[...] = jnp.broadcast_to(total, (slots, LANES)).astype(bf16)


def route(z, pieces, column):
    whole = pl.BlockSpec((SLOTS, RING * LANES), lambda i: (0, 0))
    codes = [
        pl.BlockSpec((LANES, LANES), lambda i, at=column if piece.shape[1] > LANES else 0: (0, at // LANES))
        for piece in pieces
    ]
    return pl.pallas_call(
        route_kernel,
        grid=(1,),
        out_shape=(
            jax.ShapeDtypeStruct((SLOTS, RING * LANES), bf16),
            jax.ShapeDtypeStruct((SLOTS, LANES), bf16),
        ),
        in_specs=[pl.BlockSpec(memory_space=pltpu.SMEM)] + codes,
        out_specs=(whole, pl.BlockSpec((SLOTS, LANES), lambda i: (0, 0))),
        compiler_params=pltpu.CompilerParams(vmem_limit_bytes=VMEM_LIMIT),
        cost_estimate=pl.CostEstimate(flops=10**8, bytes_accessed=2 * 10**6, transcendentals=0),
        name="route",
    )(z, *pieces)


def pack_kernel(halfway, select_ref, gate_ref, *refs):
    pieces, (first_ref, second_ref), out_ref = refs[: RING - 1], refs[RING - 1 : RING + 1], refs[-1]
    middle = RING // 2
    step = pl.program_id(0)

    @pl.when(step < 2 * halfway)
    def _():
        far = jnp.where(step < halfway, first_ref[...], second_ref[...])
        rows = [piece[...] for piece in pieces]
        rows = jnp.concatenate(rows[:middle] + [far] + rows[middle:], axis=0)
        out_ref[...] = jnp.dot(select_ref[...], rows, preferred_element_type=f32).astype(bf16)

    @pl.when(step == 2 * halfway)
    def _():
        out_ref[:, :LANES] = gate_ref[...]


def pack(select, gate_column, pieces, first, second):
    tile = 384
    halfway = RING_SPLIT // tile
    width = 2 * RING_SPLIT
    near = pl.BlockSpec((LANES, tile), lambda i: (0, jnp.minimum(i, 2 * halfway - 1)))
    middle = RING // 2
    return pl.pallas_call(
        functools.partial(pack_kernel, halfway),
        grid=(2 * halfway + 1,),
        out_shape=jax.ShapeDtypeStruct((SLOTS, width + LANES), bf16),
        in_specs=[
            pl.BlockSpec((SLOTS, RING * LANES), lambda i: (0, 0)),
            pl.BlockSpec((SLOTS, LANES), lambda i: (0, 0)),
        ]
        + [near] * (RING - 1)
        + [
            pl.BlockSpec((LANES, tile), lambda i: (0, jnp.minimum(i, halfway - 1))),
            pl.BlockSpec((LANES, tile), lambda i: (0, jnp.clip(i - halfway, 0, halfway - 1))),
        ],
        out_specs=pl.BlockSpec((SLOTS, tile), lambda i: (0, i)),
        compiler_params=pltpu.CompilerParams(vmem_limit_bytes=VMEM_LIMIT),
        cost_estimate=pl.CostEstimate(
            flops=2 * SLOTS * RING * LANES * width,
            bytes_accessed=2 * width * (SLOTS + RING * LANES) + 2 * SLOTS * RING * LANES,
            transcendentals=0,
        ),
        name="pack",
    )(select, gate_column, *pieces[:middle], *pieces[middle + 1 :], first, second)


def ranks(code):
    expert = lax.broadcasted_iota(jnp.int32, (LANES, LANES), 0).astype(f32)
    match = jnp.zeros((LANES, LANES), f32)
    for k in range(TOPK):
        match = match + jnp.where(expert == code[k : k + 1], 1.0, 0.0)
    before = (
        lax.broadcasted_iota(jnp.int32, (LANES, LANES), 0)
        < lax.broadcasted_iota(jnp.int32, (LANES, LANES), 1)
    ).astype(bf16)
    return expert, match, jnp.dot(match.astype(bf16), before, preferred_element_type=f32)


def choose(code):
    unused, match, rank = ranks(code)
    order = (match * (rank + 1.0)).astype(bf16)
    row = lax.broadcasted_iota(jnp.int32, (SLOTS, LANES), 0)
    spread = (row // CAP == lax.broadcasted_iota(jnp.int32, (SLOTS, LANES), 1)).astype(bf16)
    order = jnp.dot(spread, order, preferred_element_type=f32)
    return order == (row % CAP + 1).astype(f32)


def own_kernel(info_ref, x_ref, *refs):
    out_ref, chosen_ref = refs[-2:]

    @pl.when(pl.program_id(0) == 0)
    def _():
        chosen = choose(info_ref[...].astype(f32).T[:TOPK])
        chosen_ref[...] = jnp.where(chosen, 1.0, 0.0).astype(bf16)

    out_ref[...] = jnp.dot(chosen_ref[...], x_ref[...], preferred_element_type=f32).astype(bf16)


def own_slots(info, x, later):
    width = x.shape[1]
    tile = 256
    return pl.pallas_call(
        own_kernel,
        grid=(width // tile,),
        out_shape=jax.ShapeDtypeStruct((SLOTS, width), bf16),
        in_specs=[
            pl.BlockSpec((LANES, LANES), lambda i: (0, 0)),
            pl.BlockSpec((LANES, tile), lambda i: (0, i)),
        ]
        + [pl.BlockSpec(memory_space=pl.ANY)] * len(later),
        out_specs=pl.BlockSpec((SLOTS, tile), lambda i: (0, i)),
        scratch_shapes=[pltpu.VMEM((SLOTS, LANES), bf16)],
        compiler_params=pltpu.CompilerParams(vmem_limit_bytes=VMEM_LIMIT),
        cost_estimate=pl.CostEstimate(
            flops=2 * SLOTS * LANES * width, bytes_accessed=2 * SLOTS * width, transcendentals=0
        ),
        name="own_slots",
    )(info, x, *later)


def moved_rows(z, turned):
    place = lax.broadcasted_iota(jnp.int32, (SLOTS, SLOTS), 0 if turned else 1)
    moved = lax.broadcasted_iota(jnp.int32, (SLOTS, SLOTS), 1 if turned else 0)
    step, rest = moved // (NODES * CAP), moved % (NODES * CAP)
    at = lax.rem(z + (RING - step if turned else step), RING)
    return jnp.where(place == rest // CAP * BLOCK + at * CAP + rest % CAP, 1.0, 0.0).astype(bf16)


def turn_kernel(z_ref, x_ref, *refs):
    outs, move_ref = refs[:-1], refs[-1]

    @pl.when(pl.program_id(0) == 0)
    def _():
        move_ref[...] = moved_rows(z_ref[0], False)

    rows = jnp.dot(move_ref[...], x_ref[...], preferred_element_type=f32).astype(bf16)
    part, middle = NODES * CAP, RING // 2
    blocks = [rows[k * part : (k + 1) * part] for k in range(RING)]
    blocks[2] = jnp.concatenate([blocks[2], blocks[middle][: part // 2]], axis=0)
    blocks[-2] = jnp.concatenate([blocks[-2], blocks[middle][part // 2 :]], axis=0)
    for out, block in zip(outs, blocks[:middle] + blocks[middle + 1 :]):
        out[...] = block


def turn(z, x):
    width = x.shape[1]
    tile = 256
    part = NODES * CAP
    heights = [part, part, part + part // 2, part, part, part + part // 2, part]
    return pl.pallas_call(
        turn_kernel,
        grid=(width // tile,),
        out_shape=[jax.ShapeDtypeStruct((height, width), bf16) for height in heights],
        in_specs=[
            pl.BlockSpec(memory_space=pltpu.SMEM),
            pl.BlockSpec((SLOTS, tile), lambda i: (0, i)),
        ],
        out_specs=[pl.BlockSpec((height, tile), lambda i: (0, i)) for height in heights],
        scratch_shapes=[pltpu.VMEM((SLOTS, SLOTS), bf16)],
        compiler_params=pltpu.CompilerParams(vmem_limit_bytes=VMEM_LIMIT),
        cost_estimate=pl.CostEstimate(
            flops=2 * SLOTS * SLOTS * width, bytes_accessed=4 * SLOTS * width, transcendentals=0
        ),
        name="turn",
    )(z, x)


def cross(blocks):
    def step(x, k):
        return lax.ppermute(x, "local", [(i, (i + k) % RING) for i in range(RING)])

    part = NODES * CAP
    zero, one, two, three, back3, back2, back1 = blocks
    two, back2 = step(two, 2), step(back2, -2)
    ahead, behind = step(two[part:], 2), step(back2[part:], -2)
    return [zero, step(one, 1), two, step(three, 3), ahead, behind, step(back3, -3), back2, step(back1, -1)]


def settle_kernel(z_ref, *refs):
    pieces, out_ref, move_ref = refs[:-2], refs[-2], refs[-1]

    @pl.when(pl.program_id(0) == 0)
    def _():
        move_ref[...] = moved_rows(z_ref[0], True)

    rows = jnp.concatenate([piece[...] for piece in pieces], axis=0)
    out_ref[...] = jnp.dot(move_ref[...], rows, preferred_element_type=f32).astype(bf16)


def settle(z, pieces):
    width = pieces[0].shape[1]
    tile = 256
    return pl.pallas_call(
        settle_kernel,
        grid=(width // tile,),
        out_shape=jax.ShapeDtypeStruct((SLOTS, width), bf16),
        in_specs=[pl.BlockSpec(memory_space=pltpu.SMEM)]
        + [
            pl.BlockSpec((min(piece.shape[0], NODES * CAP), tile), lambda i: (0, i))
            for piece in pieces
        ],
        out_specs=pl.BlockSpec((SLOTS, tile), lambda i: (0, i)),
        scratch_shapes=[pltpu.VMEM((SLOTS, SLOTS), bf16)],
        compiler_params=pltpu.CompilerParams(vmem_limit_bytes=VMEM_LIMIT),
        cost_estimate=pl.CostEstimate(
            flops=2 * SLOTS * SLOTS * width, bytes_accessed=4 * SLOTS * width, transcendentals=0
        ),
        name="settle",
    )(z, *pieces)


def halves_kernel(up_ref, down_ref, *refs):
    refs[-2][...] = up_ref[...]
    refs[-1][...] = down_ref[...]


def halves(up, down, later):
    tile = 384
    steps = RING_SPLIT // tile
    line = lambda i: (0, i)
    return pl.pallas_call(
        halves_kernel,
        grid=(steps,),
        out_shape=(jax.ShapeDtypeStruct((LANES, RING_SPLIT), bf16),) * 2,
        in_specs=[
            pl.BlockSpec((LANES, tile), line),
            pl.BlockSpec((LANES, tile), lambda i: (0, i + steps)),
        ]
        + [pl.BlockSpec(memory_space=pl.ANY)] * len(later),
        out_specs=(pl.BlockSpec((LANES, tile), line),) * 2,
        compiler_params=pltpu.CompilerParams(vmem_limit_bytes=VMEM_LIMIT),
        cost_estimate=pl.CostEstimate(flops=0, bytes_accessed=10**6, transcendentals=0),
        name="halves",
    )(up, down, *later)


def ring(block):
    ahead = [(i, (i + 1) % RING) for i in range(RING)]
    back = [(i, (i - 1) % RING) for i in range(RING)]
    pieces = [block] + [None] * (RING - 1)
    up = down = block
    for step in range(1, RING // 2):
        up = lax.ppermute(up, "local", ahead)
        down = lax.ppermute(down, "local", back)
        pieces[step], pieces[RING - step] = up, down
    return pieces


def farthest(up, down, later):
    ahead = [(i, (i + 1) % RING) for i in range(RING)]
    back = [(i, (i - 1) % RING) for i in range(RING)]
    first, second = halves(up, down, later)
    return lax.ppermute(first, "local", ahead), lax.ppermute(second, "local", back)


def back_kernel(half, rows_ref, acc_ref, hidden_ref, other_ref, own_ref, grad_ref, sums_ref, gated_ref):
    wide = half + own_ref.shape[0]
    total = acc_ref[...]
    total = total + jnp.dot(rows_ref[:, :half], other_ref[...], preferred_element_type=f32)
    total = total + jnp.dot(rows_ref[:, half:wide], own_ref[...], preferred_element_type=f32)
    gate = rows_ref[:, wide : wide + 1].astype(f32)
    hidden = hidden_ref[...].astype(f32)
    grad_ref[...] = (gate * total).astype(bf16)
    gated_ref[...] = (gate * hidden).astype(bf16)
    sums_ref[...] = jnp.sum(hidden * total, axis=1, keepdims=True)


def back(rows, acc, hidden, weight_other, weight_own, rest):
    tile = 192
    half, units = weight_other.shape
    line = lambda i: (i, 0)
    still = lambda i: (0, 0)
    return pl.pallas_call(
        functools.partial(back_kernel, half),
        grid=(SLOTS // tile,),
        out_shape=(
            jax.ShapeDtypeStruct((SLOTS, units), bf16),
            jax.ShapeDtypeStruct((SLOTS, 1), f32),
            jax.ShapeDtypeStruct((SLOTS, units), bf16),
        ),
        in_specs=[
            pl.BlockSpec((tile, rows.shape[1]), line),
            pl.BlockSpec((tile, units), line),
            pl.BlockSpec((tile, units), line),
            pl.BlockSpec((half, units), still),
            pl.BlockSpec((rest, units), still),
        ],
        out_specs=(
            pl.BlockSpec((tile, units), line),
            pl.BlockSpec((tile, 1), line),
            pl.BlockSpec((tile, units), line),
        ),
        compiler_params=pltpu.CompilerParams(vmem_limit_bytes=24 * 2**20),
        cost_estimate=pl.CostEstimate(
            flops=2 * SLOTS * units * (half + rest), bytes_accessed=16 * 10**6, transcendentals=0
        ),
        name="back",
    )(rows, acc, hidden, weight_other, weight_own)


def down_kernel(steps, x_ref, y_ref, gated_ref, received_ref, out_ref):
    step = pl.program_id(0)
    rows = jnp.where(step < steps, x_ref[...], y_ref[...])
    share = lax.dot_general(rows, gated_ref[...], (((0,), (0,)), ((), ())), preferred_element_type=f32)
    out_ref[...] = (share + received_ref[...].astype(f32)).astype(bf16)


def down(x, skip, y, gated, received):
    tile = 256
    steps = (x.shape[1] - skip) // tile
    more = y.shape[1] // tile
    units = gated.shape[1]
    return pl.pallas_call(
        functools.partial(down_kernel, steps),
        grid=(steps + more,),
        out_shape=jax.ShapeDtypeStruct(received.shape, bf16),
        in_specs=[
            pl.BlockSpec((SLOTS, tile), lambda i: (0, skip // tile + jnp.minimum(i, steps - 1))),
            pl.BlockSpec((SLOTS, tile), lambda i: (0, jnp.maximum(i - steps, 0))),
            pl.BlockSpec((SLOTS, units), lambda i: (0, 0)),
            pl.BlockSpec((tile, units), lambda i: (i, 0)),
        ],
        out_specs=pl.BlockSpec((tile, units), lambda i: (i, 0)),
        compiler_params=pltpu.CompilerParams(vmem_limit_bytes=VMEM_LIMIT),
        cost_estimate=pl.CostEstimate(
            flops=2 * SLOTS * units * received.shape[0], bytes_accessed=12 * 10**6, transcendentals=0
        ),
        name="down",
    )(x, y, gated, received)


def finish_kernel(info_ref, logits_ref, value_ref, *refs):
    out_ref = refs[-1]
    code = info_ref[...].astype(f32).T[:TOPK]
    expert, match, rank = ranks(code)
    value = jnp.zeros((LANES, LANES), f32)
    for c in range(CAP):
        value = jnp.where(rank == float(c), value_ref[:, c : c + 1], value)
    value = jnp.where(match > 0.0, value, 0.0)
    pairs = [
        jnp.sum(jnp.where(expert == code[k : k + 1], value, 0.0), axis=0, keepdims=True)
        for k in range(TOPK)
    ]
    pair_grad = jnp.concatenate(pairs, axis=0)
    affinity = 1.0 / (1.0 + jnp.exp(-logits_ref[...]))
    denominator = jnp.sum(affinity, axis=0, keepdims=True)
    weighted = jnp.sum(pair_grad * affinity, axis=0, keepdims=True)
    grad = route_scale * (pair_grad / denominator - weighted / (denominator * denominator))
    out_ref[...] = grad * affinity * (1.0 - affinity)


def finish(info, logits, value, later):
    vmem = pl.BlockSpec(memory_space=pltpu.VMEM)
    return pl.pallas_call(
        finish_kernel,
        out_shape=jax.ShapeDtypeStruct(logits.shape, f32),
        in_specs=[vmem] * 3 + [pl.BlockSpec(memory_space=pl.ANY)] * len(later),
        out_specs=vmem,
        compiler_params=pltpu.CompilerParams(vmem_limit_bytes=VMEM_LIMIT),
        cost_estimate=pl.CostEstimate(flops=10**7, bytes_accessed=10**6, transcendentals=10**4),
        name="finish",
    )(info, logits, value, *later)


def local(out_grad, expert_ids, drop_flags, router_logits, saved_hidden, down_weight):
    slot_total = saved_hidden.shape[2]
    tok_rows = out_grad.shape[0]
    top_count = expert_ids.shape[1]
    half = out_grad.shape[1] // 2
    experts = NODES * RING
    z = lax.axis_index("local")
    copy = lax.axis_index("replica")
    swap = [(0, 1), (1, 0)]

    affinity = jax.nn.sigmoid(router_logits)
    denominator = jnp.sum(affinity, axis=1, keepdims=True)
    gate_sent = (route_scale * affinity / denominator).astype(bf16)
    code = jnp.where(drop_flags == 0, expert_ids, -1).astype(bf16)
    info = jnp.concatenate([code, gate_sent], axis=1)
    info = jnp.pad(info, ((0, 0), (0, LANES - 2 * top_count)))

    weight_own = down_weight.reshape(half, down_weight.shape[2])
    weight_other = lax.ppermute(weight_own, "replica", swap)
    hidden = saved_hidden.reshape(slot_total, saved_hidden.shape[3])

    low, high = out_grad[:, :half], out_grad[:, half:]
    other, own = jnp.where(copy == 0, high, low), jnp.where(copy == 0, low, high)
    at = z.reshape(1)
    rest = half - EARLY
    wide = half + rest

    middle = RING // 2
    pieces = ring(jnp.concatenate([other, own[:, :rest], info], axis=1))
    far_info = lax.ppermute(info, "local", [(i, (i + middle) % RING) for i in range(RING)])

    early = own_slots(info, own[:, rest:], ())
    early = early.reshape(NODES, BLOCK, EARLY)
    early = lax.all_to_all(early, "node", split_axis=0, concat_axis=0, tiled=True)
    early = turn(at, early.reshape(slot_total, EARLY))
    first, second = farthest(pieces[middle - 1], pieces[middle + 1], (early[0],))
    crossed = cross(early)
    select, gate_column = route(at, pieces[:middle] + [far_info] + pieces[middle + 1 :], wide)
    rows = pack(select, gate_column, pieces, first, second)
    rows = rows.reshape(NODES, BLOCK, wide + LANES)
    rows = lax.all_to_all(rows, "node", split_axis=0, concat_axis=0, tiled=True)
    rows = rows.reshape(slot_total, wide + LANES)

    early = settle(at, crossed)
    acc = jnp.dot(early, weight_own[rest:], preferred_element_type=f32)
    grad_hidden, gate_grad, gated = back(rows, acc, hidden, weight_other, weight_own, rest)
    grad_hidden = grad_hidden.reshape(saved_hidden.shape)
    returned = lax.all_to_all(
        gate_grad.reshape(experts, CAP),
        ("node", "local"),
        split_axis=0,
        concat_axis=0,
        tiled=True,
    )
    received = lax.dot_general(
        rows[:, :half], gated, (((0,), (0,)), ((), ())), preferred_element_type=f32
    )
    received = lax.ppermute(received.astype(bf16), "replica", swap)
    grad_down = down(rows[:, half:wide], 0, early, gated, received)
    grad_logits = finish(info, router_logits.T, returned, (grad_down,)).T
    return (grad_logits, grad_hidden, grad_down.reshape(down_weight.shape))


def solution(mesh):
    return jax.shard_map(
        local,
        mesh=mesh,
        in_specs=(
            P(("node", "local", "replica"), None),
            P(("node", "local", "replica"), None),
            P(("node", "local", "replica"), None),
            P(("node", "local", "replica"), None),
            P("replica", ("node", "local"), None, None),
            P(("node", "local"), "replica", None),
        ),
        out_specs=(
            P(("node", "local", "replica"), None),
            P("replica", ("node", "local"), None, None),
            P(("node", "local"), "replica", None),
        ),
        check_vma=False,
    )
```

```python
import functools

import jax
import jax.numpy as jnp
from jax import lax
from jax.experimental import pallas as pl
from jax.experimental.pallas import tpu as pltpu
from jax.sharding import PartitionSpec as P

route_scale = 2.5
bf16 = jnp.bfloat16
f32 = jnp.float32
EARLY = 1280
NODES = 16
RING = 8
CAP = 6
TOPK = 8
BLOCK = RING * CAP
LANES = 128
SLOTS = NODES * BLOCK
RING_SPLIT = 1152
VMEM_LIMIT = 14 * 2**20


def codes_kernel(ids_ref, drop_ref, logits_ref, out_ref):
    code = jnp.where(drop_ref[...] == 0, ids_ref[...], -1).astype(f32)
    affinity = 1.0 / (1.0 + jnp.exp(-logits_ref[...]))
    gate = route_scale * affinity / jnp.sum(affinity, axis=0, keepdims=True)
    rest = jnp.zeros((LANES - 2 * TOPK, LANES), f32)
    out_ref[...] = jnp.concatenate([code, gate, rest], axis=0).T.astype(bf16)


def codes(expert_ids, drop_flags, router_logits):
    vmem = pl.BlockSpec(memory_space=pltpu.VMEM)
    return pl.pallas_call(
        codes_kernel,
        out_shape=jax.ShapeDtypeStruct((LANES, LANES), bf16),
        in_specs=[vmem] * 3,
        out_specs=vmem,
        compiler_params=pltpu.CompilerParams(vmem_limit_bytes=VMEM_LIMIT),
        cost_estimate=pl.CostEstimate(flops=10**5, bytes_accessed=10**5, transcendentals=10**3),
        name="codes",
    )(expert_ids.T, drop_flags.T, router_logits.T)


def route_kernel(z_ref, *refs):
    infos, (select_ref, gate_ref) = refs[:RING], refs[RING:]
    slots = SLOTS
    z = z_ref[0]
    expert = (lax.broadcasted_iota(jnp.int32, (NODES, LANES), 0) * RING + z).astype(f32)
    before = (
        lax.broadcasted_iota(jnp.int32, (LANES, LANES), 0)
        < lax.broadcasted_iota(jnp.int32, (LANES, LANES), 1)
    ).astype(bf16)
    spread = (
        lax.broadcasted_iota(jnp.int32, (slots, NODES), 0) // BLOCK
        == lax.broadcasted_iota(jnp.int32, (slots, NODES), 1)
    ).astype(bf16)
    row = lax.broadcasted_iota(jnp.int32, (slots, LANES), 0) % BLOCK
    source = row // CAP
    wanted = (row % CAP + 1).astype(f32)
    slot_gate = jnp.zeros((slots, LANES), f32)
    for j in range(RING):
        info = infos[j][...].astype(f32).T
        code, gate = info[:TOPK], info[TOPK : 2 * TOPK]
        match = jnp.zeros((NODES, LANES), f32)
        match_gate = jnp.zeros((NODES, LANES), f32)
        for k in range(TOPK):
            hit = expert == code[k : k + 1]
            match = match + jnp.where(hit, 1.0, 0.0)
            match_gate = match_gate + jnp.where(hit, gate[k : k + 1], 0.0)
        rank = jnp.dot(match.astype(bf16), before, preferred_element_type=f32)
        order = (match * (rank + 1.0)).astype(bf16)
        order = jnp.dot(spread, order, preferred_element_type=f32)
        spread_gate = jnp.dot(spread, match_gate.astype(bf16), preferred_element_type=f32)
        origin = lax.rem(z + RING - j, RING)
        here = (order == wanted) & (source == origin)
        block = jnp.where(here, 1.0, 0.0).astype(bf16)
        select_ref[:, j * LANES : (j + 1) * LANES] = block
        slot_gate = slot_gate + jnp.where(here, spread_gate, 0.0)
    total = jnp.sum(slot_gate, axis=1, keepdims=True)
    gate_ref[...] = jnp.broadcast_to(total, (slots, LANES)).astype(bf16)


def route(z, pieces, column):
    whole = pl.BlockSpec((SLOTS, RING * LANES), lambda i: (0, 0))
    blocks = [
        pl.BlockSpec((LANES, LANES), lambda i, at=column if piece.shape[1] > LANES else 0: (0, at // LANES))
        for piece in pieces
    ]
    return pl.pallas_call(
        route_kernel,
        grid=(1,),
        out_shape=(
            jax.ShapeDtypeStruct((SLOTS, RING * LANES), bf16),
            jax.ShapeDtypeStruct((SLOTS, LANES), bf16),
        ),
        in_specs=[pl.BlockSpec(memory_space=pltpu.SMEM)] + blocks,
        out_specs=(whole, pl.BlockSpec((SLOTS, LANES), lambda i: (0, 0))),
        compiler_params=pltpu.CompilerParams(vmem_limit_bytes=VMEM_LIMIT),
        cost_estimate=pl.CostEstimate(flops=10**8, bytes_accessed=2 * 10**6, transcendentals=0),
        name="route",
    )(z, *pieces)


def pack_kernel(halfway, select_ref, gate_ref, *refs):
    pieces, (first_ref, second_ref), out_ref = refs[: RING - 1], refs[RING - 1 : RING + 1], refs[-1]
    middle = RING // 2
    step = pl.program_id(0)

    @pl.when(step < 2 * halfway)
    def _():
        far = jnp.where(step < halfway, first_ref[...], second_ref[...])
        rows = [piece[...] for piece in pieces]
        rows = jnp.concatenate(rows[:middle] + [far] + rows[middle:], axis=0)
        out_ref[...] = jnp.dot(select_ref[...], rows, preferred_element_type=f32).astype(bf16)

    @pl.when(step == 2 * halfway)
    def _():
        out_ref[:, :LANES] = gate_ref[...]


def pack(select, gate_column, pieces, first, second):
    tile = 384
    halfway = RING_SPLIT // tile
    width = 2 * RING_SPLIT
    near = pl.BlockSpec((LANES, tile), lambda i: (0, jnp.minimum(i, 2 * halfway - 1)))
    middle = RING // 2
    return pl.pallas_call(
        functools.partial(pack_kernel, halfway),
        grid=(2 * halfway + 1,),
        out_shape=pltpu.HBM((SLOTS, width + LANES), bf16),
        in_specs=[
            pl.BlockSpec((SLOTS, RING * LANES), lambda i: (0, 0)),
            pl.BlockSpec((SLOTS, LANES), lambda i: (0, 0)),
        ]
        + [near] * (RING - 1)
        + [
            pl.BlockSpec((LANES, tile), lambda i: (0, jnp.minimum(i, halfway - 1))),
            pl.BlockSpec((LANES, tile), lambda i: (0, jnp.clip(i - halfway, 0, halfway - 1))),
        ],
        out_specs=pl.BlockSpec((SLOTS, tile), lambda i: (0, i)),
        compiler_params=pltpu.CompilerParams(vmem_limit_bytes=VMEM_LIMIT),
        cost_estimate=pl.CostEstimate(
            flops=2 * SLOTS * RING * LANES * width,
            bytes_accessed=2 * width * (SLOTS + RING * LANES) + 2 * SLOTS * RING * LANES,
            transcendentals=0,
        ),
        name="pack",
    )(select, gate_column, *pieces[:middle], *pieces[middle + 1 :], first, second)


def ranks(code):
    expert = lax.broadcasted_iota(jnp.int32, (LANES, LANES), 0).astype(f32)
    match = jnp.zeros((LANES, LANES), f32)
    for k in range(TOPK):
        match = match + jnp.where(expert == code[k : k + 1], 1.0, 0.0)
    before = (
        lax.broadcasted_iota(jnp.int32, (LANES, LANES), 0)
        < lax.broadcasted_iota(jnp.int32, (LANES, LANES), 1)
    ).astype(bf16)
    return expert, match, jnp.dot(match.astype(bf16), before, preferred_element_type=f32)


def choose(code):
    unused, match, rank = ranks(code)
    order = (match * (rank + 1.0)).astype(bf16)
    row = lax.broadcasted_iota(jnp.int32, (SLOTS, LANES), 0)
    spread = (row // CAP == lax.broadcasted_iota(jnp.int32, (SLOTS, LANES), 1)).astype(bf16)
    order = jnp.dot(spread, order, preferred_element_type=f32)
    return order == (row % CAP + 1).astype(f32)


def own_kernel(info_ref, x_ref, *refs):
    out_ref, chosen_ref = refs[-2:]

    @pl.when(pl.program_id(0) == 0)
    def _():
        chosen = choose(info_ref[...].astype(f32).T[:TOPK])
        chosen_ref[...] = jnp.where(chosen, 1.0, 0.0).astype(bf16)

    out_ref[...] = jnp.dot(chosen_ref[...], x_ref[...], preferred_element_type=f32).astype(bf16)


def own_slots(info, x, later):
    width = x.shape[1]
    tile = 256
    return pl.pallas_call(
        own_kernel,
        grid=(width // tile,),
        out_shape=jax.ShapeDtypeStruct((SLOTS, width), bf16),
        in_specs=[
            pl.BlockSpec((LANES, LANES), lambda i: (0, 0)),
            pl.BlockSpec((LANES, tile), lambda i: (0, i)),
        ]
        + [pl.BlockSpec(memory_space=pl.ANY)] * len(later),
        out_specs=pl.BlockSpec((SLOTS, tile), lambda i: (0, i)),
        scratch_shapes=[pltpu.VMEM((SLOTS, LANES), bf16)],
        compiler_params=pltpu.CompilerParams(vmem_limit_bytes=VMEM_LIMIT),
        cost_estimate=pl.CostEstimate(
            flops=2 * SLOTS * LANES * width, bytes_accessed=2 * SLOTS * width, transcendentals=0
        ),
        name="own_slots",
    )(info, x, *later)


def moved_rows(z, turned):
    place = lax.broadcasted_iota(jnp.int32, (SLOTS, SLOTS), 0 if turned else 1)
    moved = lax.broadcasted_iota(jnp.int32, (SLOTS, SLOTS), 1 if turned else 0)
    step, rest = moved // (NODES * CAP), moved % (NODES * CAP)
    at = lax.rem(z + (RING - step if turned else step), RING)
    return jnp.where(place == rest // CAP * BLOCK + at * CAP + rest % CAP, 1.0, 0.0).astype(bf16)


def turn_kernel(z_ref, x_ref, *refs):
    outs, move_ref = refs[:-1], refs[-1]

    @pl.when(pl.program_id(0) == 0)
    def _():
        move_ref[...] = moved_rows(z_ref[0], False)

    rows = jnp.dot(move_ref[...], x_ref[...], preferred_element_type=f32).astype(bf16)
    part, middle = NODES * CAP, RING // 2
    blocks = [rows[k * part : (k + 1) * part] for k in range(RING)]
    blocks[2] = jnp.concatenate([blocks[2], blocks[middle][: part // 2]], axis=0)
    blocks[-2] = jnp.concatenate([blocks[-2], blocks[middle][part // 2 :]], axis=0)
    for out, block in zip(outs, blocks[:middle] + blocks[middle + 1 :]):
        out[...] = block


def turn(z, x):
    width = x.shape[1]
    tile = 256
    part = NODES * CAP
    heights = [part, part, part + part // 2, part, part, part + part // 2, part]
    return pl.pallas_call(
        turn_kernel,
        grid=(width // tile,),
        out_shape=[jax.ShapeDtypeStruct((height, width), bf16) for height in heights],
        in_specs=[
            pl.BlockSpec(memory_space=pltpu.SMEM),
            pl.BlockSpec((SLOTS, tile), lambda i: (0, i)),
        ],
        out_specs=[pl.BlockSpec((height, tile), lambda i: (0, i)) for height in heights],
        scratch_shapes=[pltpu.VMEM((SLOTS, SLOTS), bf16)],
        compiler_params=pltpu.CompilerParams(vmem_limit_bytes=VMEM_LIMIT),
        cost_estimate=pl.CostEstimate(
            flops=2 * SLOTS * SLOTS * width, bytes_accessed=4 * SLOTS * width, transcendentals=0
        ),
        name="turn",
    )(z, x)


def cross(blocks):
    def step(x, k):
        return lax.ppermute(x, "local", [(i, (i + k) % RING) for i in range(RING)])

    part = NODES * CAP
    zero, one, two, three, back3, back2, back1 = blocks
    two, back2 = step(two, 2), step(back2, -2)
    ahead, behind = step(two[part:], 2), step(back2[part:], -2)
    return [zero, step(one, 1), two, step(three, 3), ahead, behind, step(back3, -3), back2, step(back1, -1)]


def settle_kernel(z_ref, *refs):
    pieces, out_ref, move_ref = refs[:-2], refs[-2], refs[-1]

    @pl.when(pl.program_id(0) == 0)
    def _():
        move_ref[...] = moved_rows(z_ref[0], True)

    rows = jnp.concatenate([piece[...] for piece in pieces], axis=0)
    out_ref[...] = jnp.dot(move_ref[...], rows, preferred_element_type=f32).astype(bf16)


def settle(z, pieces):
    width = pieces[0].shape[1]
    tile = 256
    return pl.pallas_call(
        settle_kernel,
        grid=(width // tile,),
        out_shape=jax.ShapeDtypeStruct((SLOTS, width), bf16),
        in_specs=[pl.BlockSpec(memory_space=pltpu.SMEM)]
        + [
            pl.BlockSpec((min(piece.shape[0], NODES * CAP), tile), lambda i: (0, i))
            for piece in pieces
        ],
        out_specs=pl.BlockSpec((SLOTS, tile), lambda i: (0, i)),
        scratch_shapes=[pltpu.VMEM((SLOTS, SLOTS), bf16)],
        compiler_params=pltpu.CompilerParams(vmem_limit_bytes=VMEM_LIMIT),
        cost_estimate=pl.CostEstimate(
            flops=2 * SLOTS * SLOTS * width, bytes_accessed=4 * SLOTS * width, transcendentals=0
        ),
        name="settle",
    )(z, *pieces)


def halves_kernel(up_ref, down_ref, *refs):
    refs[-2][...] = up_ref[...]
    refs[-1][...] = down_ref[...]


def halves(up, down, later):
    tile = 384
    steps = RING_SPLIT // tile
    line = lambda i: (0, i)
    return pl.pallas_call(
        halves_kernel,
        grid=(steps,),
        out_shape=(jax.ShapeDtypeStruct((LANES, RING_SPLIT), bf16),) * 2,
        in_specs=[
            pl.BlockSpec((LANES, tile), line),
            pl.BlockSpec((LANES, tile), lambda i: (0, i + steps)),
        ]
        + [pl.BlockSpec(memory_space=pl.ANY)] * len(later),
        out_specs=(pl.BlockSpec((LANES, tile), line),) * 2,
        compiler_params=pltpu.CompilerParams(vmem_limit_bytes=VMEM_LIMIT),
        cost_estimate=pl.CostEstimate(flops=0, bytes_accessed=10**6, transcendentals=0),
        name="halves",
    )(up, down, *later)


def ring(block):
    ahead = [(i, (i + 1) % RING) for i in range(RING)]
    back = [(i, (i - 1) % RING) for i in range(RING)]
    pieces = [block] + [None] * (RING - 1)
    up = down = block
    for step in range(1, RING // 2):
        up = lax.ppermute(up, "local", ahead)
        down = lax.ppermute(down, "local", back)
        pieces[step], pieces[RING - step] = up, down
    return pieces


def farthest(up, down, later):
    ahead = [(i, (i + 1) % RING) for i in range(RING)]
    back = [(i, (i - 1) % RING) for i in range(RING)]
    first, second = halves(up, down, later)
    return lax.ppermute(first, "local", ahead), lax.ppermute(second, "local", back)


def back_kernel(rest, rows_ref, early_ref, hidden_ref, other_ref, own_ref, grad_ref, sums_ref, gated_ref):
    half = other_ref.shape[0]
    wide = half + rest
    total = jnp.dot(rows_ref[:, :half], other_ref[...], preferred_element_type=f32)
    total = total + jnp.dot(rows_ref[:, half:wide], own_ref[:rest], preferred_element_type=f32)
    total = total + jnp.dot(early_ref[...], own_ref[rest:], preferred_element_type=f32)
    gate = rows_ref[:, wide : wide + 1].astype(f32)
    hidden = hidden_ref[...].astype(f32)
    grad_ref[...] = (gate * total).astype(bf16)
    gated_ref[...] = (gate * hidden).astype(bf16)
    tile = rows_ref.shape[0]
    sums = jnp.sum(hidden * total, axis=1, keepdims=True)
    lane = lax.broadcasted_iota(jnp.int32, (tile, LANES), 1)
    rank = lax.broadcasted_iota(jnp.int32, (tile, LANES), 0) % CAP
    expert = lax.broadcasted_iota(jnp.int32, (tile // CAP, tile), 0)
    gather = jnp.where(expert == lax.broadcasted_iota(jnp.int32, expert.shape, 1) // CAP, 1.0, 0.0)
    sums_ref[...] = jnp.dot(
        gather,
        jnp.where(lane == rank, sums, 0.0),
        precision=lax.Precision.HIGHEST,
        preferred_element_type=f32,
    )


def back(rows, early, hidden, weight_other, weight_own):
    tile = 384
    half, units = weight_other.shape
    line = lambda i: (i, 0)
    still = pl.BlockSpec((half, units), lambda i: (0, 0), pipeline_mode=pl.Buffered(1))
    return pl.pallas_call(
        functools.partial(back_kernel, half - early.shape[1]),
        grid=(SLOTS // tile,),
        out_shape=(
            jax.ShapeDtypeStruct((SLOTS, units), bf16),
            jax.ShapeDtypeStruct((SLOTS // CAP, LANES), f32),
            jax.ShapeDtypeStruct((SLOTS, units), bf16),
        ),
        in_specs=[
            pl.BlockSpec((tile, rows.shape[1]), line),
            pl.BlockSpec((tile, early.shape[1]), line),
            pl.BlockSpec((tile, units), line),
            still,
            still,
        ],
        out_specs=(
            pl.BlockSpec((tile, units), line),
            pl.BlockSpec((tile // CAP, LANES), line),
            pl.BlockSpec((tile, units), line),
        ),
        compiler_params=pltpu.CompilerParams(vmem_limit_bytes=32 * 2**20),
        cost_estimate=pl.CostEstimate(
            flops=4 * SLOTS * units * half, bytes_accessed=18 * 10**6, transcendentals=0
        ),
        name="back",
    )(rows, early, hidden, weight_other, weight_own)


def down_kernel(steps, x_ref, y_ref, gated_ref, received_ref, out_ref, mark_ref):
    mark_ref[...] = jnp.zeros_like(mark_ref)
    step = pl.program_id(0)
    rows = jnp.where(step < steps, x_ref[...], y_ref[...])
    share = lax.dot_general(rows, gated_ref[...], (((0,), (0,)), ((), ())), preferred_element_type=f32)
    out_ref[...] = (share + received_ref[...].astype(f32)).astype(bf16)


def down(x, skip, y, gated, received):
    tile = 256
    more = y.shape[1] // tile
    steps = received.shape[0] // tile - more
    units = gated.shape[1]
    return pl.pallas_call(
        functools.partial(down_kernel, steps),
        grid=(steps + more,),
        out_shape=(
            jax.ShapeDtypeStruct(received.shape, bf16),
            jax.ShapeDtypeStruct((8, LANES), f32),
        ),
        in_specs=[
            pl.BlockSpec((SLOTS, tile), lambda i: (0, skip // tile + jnp.minimum(i, steps - 1))),
            pl.BlockSpec((SLOTS, tile), lambda i: (0, jnp.maximum(i - steps, 0))),
            pl.BlockSpec((SLOTS, units), lambda i: (0, 0)),
            pl.BlockSpec((tile, units), lambda i: (i, 0)),
        ],
        out_specs=(
            pl.BlockSpec((tile, units), lambda i: (i, 0)),
            pl.BlockSpec((8, LANES), lambda i: (0, 0)),
        ),
        compiler_params=pltpu.CompilerParams(vmem_limit_bytes=VMEM_LIMIT),
        cost_estimate=pl.CostEstimate(
            flops=2 * SLOTS * units * received.shape[0], bytes_accessed=12 * 10**6, transcendentals=0
        ),
        name="down",
    )(x, y, gated, received)


def finish_kernel(info_ref, logits_ref, value_ref, *refs):
    out_ref = refs[-1]
    code = info_ref[...].astype(f32).T[:TOPK]
    expert, match, rank = ranks(code)
    value = jnp.zeros((LANES, LANES), f32)
    for c in range(CAP):
        value = jnp.where(rank == float(c), value_ref[:, c : c + 1], value)
    value = jnp.where(match > 0.0, value, 0.0)
    pairs = [
        jnp.sum(jnp.where(expert == code[k : k + 1], value, 0.0), axis=0, keepdims=True)
        for k in range(TOPK)
    ]
    pair_grad = jnp.concatenate(pairs, axis=0)
    affinity = 1.0 / (1.0 + jnp.exp(-logits_ref[...]))
    denominator = jnp.sum(affinity, axis=0, keepdims=True)
    weighted = jnp.sum(pair_grad * affinity, axis=0, keepdims=True)
    grad = route_scale * (pair_grad / denominator - weighted / (denominator * denominator))
    out_ref[...] = grad * affinity * (1.0 - affinity)


def finish(info, logits, value, later):
    vmem = pl.BlockSpec(memory_space=pltpu.VMEM)
    return pl.pallas_call(
        finish_kernel,
        out_shape=jax.ShapeDtypeStruct(logits.shape, f32),
        in_specs=[vmem] * 3 + [pl.BlockSpec(memory_space=pl.ANY)] * len(later),
        out_specs=vmem,
        compiler_params=pltpu.CompilerParams(vmem_limit_bytes=VMEM_LIMIT),
        cost_estimate=pl.CostEstimate(flops=10**7, bytes_accessed=10**6, transcendentals=10**4),
        name="finish",
    )(info, logits, value, *later)


def local(out_grad, expert_ids, drop_flags, router_logits, saved_hidden, down_weight):
    slot_total = saved_hidden.shape[2]
    half = out_grad.shape[1] // 2
    experts = NODES * RING
    z = lax.axis_index("local")
    copy = lax.axis_index("replica")
    swap = [(0, 1), (1, 0)]

    info = codes(expert_ids, drop_flags, router_logits)

    weight_own = down_weight.reshape(half, down_weight.shape[2])
    weight_other = lax.ppermute(weight_own, "replica", swap)
    hidden = saved_hidden.reshape(slot_total, saved_hidden.shape[3])

    low, high = out_grad[:, :half], out_grad[:, half:]
    other, own = jnp.where(copy == 0, high, low), jnp.where(copy == 0, low, high)
    at = z.reshape(1)
    rest = half - EARLY
    wide = half + rest

    middle = RING // 2
    pieces = ring(jnp.concatenate([other, own[:, :rest], info], axis=1))
    far_info = lax.ppermute(info, "local", [(i, (i + middle) % RING) for i in range(RING)])

    early = own_slots(info, own[:, rest:], ())
    early = early.reshape(NODES, BLOCK, EARLY)
    early = lax.all_to_all(early, "node", split_axis=0, concat_axis=0, tiled=True)
    early = turn(at, early.reshape(slot_total, EARLY))
    first, second = farthest(pieces[middle - 1], pieces[middle + 1], ())
    crossed = cross(early)
    select, gate_column = route(at, pieces[:middle] + [far_info] + pieces[middle + 1 :], wide)
    rows = pack(select, gate_column, pieces, first, second)
    rows = rows.reshape(NODES, BLOCK, wide + LANES)
    rows = lax.all_to_all(rows, "node", split_axis=0, concat_axis=0, tiled=True)
    rows = rows.reshape(slot_total, wide + LANES)

    early = settle(at, crossed)
    grad_hidden, gate_grad, gated = back(rows, early, hidden, weight_other, weight_own)
    grad_hidden = grad_hidden.reshape(saved_hidden.shape)
    returned = lax.all_to_all(
        gate_grad[:, :CAP],
        ("node", "local"),
        split_axis=0,
        concat_axis=0,
        tiled=True,
    )
    received = lax.dot_general(
        rows[:, :half], gated, (((0,), (0,)), ((), ())), preferred_element_type=f32
    )
    received = lax.ppermute(received.astype(bf16), "replica", swap)
    grad_down, mark = down(rows, half, early, gated, received)
    grad_logits = finish(info, router_logits.T, returned, (mark,)).T
    return (grad_logits, grad_hidden, grad_down.reshape(down_weight.shape))


def solution(mesh):
    return jax.shard_map(
        local,
        mesh=mesh,
        in_specs=(
            P(("node", "local", "replica"), None),
            P(("node", "local", "replica"), None),
            P(("node", "local", "replica"), None),
            P(("node", "local", "replica"), None),
            P("replica", ("node", "local"), None, None),
            P(("node", "local"), "replica", None),
        ),
        out_specs=(
            P(("node", "local", "replica"), None),
            P("replica", ("node", "local"), None, None),
            P(("node", "local"), "replica", None),
        ),
        check_vma=False,
    )
```

```python
import functools

import jax
import jax.numpy as jnp
from jax import lax
from jax.experimental import pallas as pl
from jax.experimental.pallas import tpu as pltpu
from jax.sharding import PartitionSpec as P

route_scale = 2.5
bf16 = jnp.bfloat16
f32 = jnp.float32
EARLY = 1280
NODES = 16
RING = 8
CAP = 6
TOPK = 8
BLOCK = RING * CAP
LANES = 128
SLOTS = NODES * BLOCK
RING_SPLIT = 1152
VMEM_LIMIT = 14 * 2**20


def codes_kernel(ids_ref, drop_ref, logits_ref, out_ref):
    code = jnp.where(drop_ref[...] == 0, ids_ref[...], -1).astype(f32)
    affinity = 1.0 / (1.0 + jnp.exp(-logits_ref[...]))
    gate = route_scale * affinity / jnp.sum(affinity, axis=0, keepdims=True)
    rest = jnp.zeros((LANES - 2 * TOPK, LANES), f32)
    out_ref[...] = jnp.concatenate([code, gate, rest], axis=0).T.astype(bf16)


def codes(expert_ids, drop_flags, router_logits):
    vmem = pl.BlockSpec(memory_space=pltpu.VMEM)
    return pl.pallas_call(
        codes_kernel,
        out_shape=jax.ShapeDtypeStruct((LANES, LANES), bf16),
        in_specs=[vmem] * 3,
        out_specs=vmem,
        compiler_params=pltpu.CompilerParams(vmem_limit_bytes=VMEM_LIMIT),
        cost_estimate=pl.CostEstimate(flops=10**5, bytes_accessed=10**5, transcendentals=10**3),
        name="codes",
    )(expert_ids.T, drop_flags.T, router_logits.T)


def route_kernel(z_ref, *refs):
    infos, (select_ref, gate_ref) = refs[:RING], refs[RING:]
    slots = SLOTS
    z = z_ref[0]
    expert = (lax.broadcasted_iota(jnp.int32, (NODES, LANES), 0) * RING + z).astype(f32)
    before = (
        lax.broadcasted_iota(jnp.int32, (LANES, LANES), 0)
        < lax.broadcasted_iota(jnp.int32, (LANES, LANES), 1)
    ).astype(bf16)
    spread = (
        lax.broadcasted_iota(jnp.int32, (slots, NODES), 0) // BLOCK
        == lax.broadcasted_iota(jnp.int32, (slots, NODES), 1)
    ).astype(bf16)
    row = lax.broadcasted_iota(jnp.int32, (slots, LANES), 0) % BLOCK
    source = row // CAP
    wanted = (row % CAP + 1).astype(f32)
    slot_gate = jnp.zeros((slots, LANES), f32)
    for j in range(RING):
        info = infos[j][...].astype(f32).T
        code, gate = info[:TOPK], info[TOPK : 2 * TOPK]
        match = jnp.zeros((NODES, LANES), f32)
        match_gate = jnp.zeros((NODES, LANES), f32)
        for k in range(TOPK):
            hit = expert == code[k : k + 1]
            match = match + jnp.where(hit, 1.0, 0.0)
            match_gate = match_gate + jnp.where(hit, gate[k : k + 1], 0.0)
        rank = jnp.dot(match.astype(bf16), before, preferred_element_type=f32)
        order = (match * (rank + 1.0)).astype(bf16)
        order = jnp.dot(spread, order, preferred_element_type=f32)
        spread_gate = jnp.dot(spread, match_gate.astype(bf16), preferred_element_type=f32)
        origin = lax.rem(z + RING - j, RING)
        here = (order == wanted) & (source == origin)
        block = jnp.where(here, 1.0, 0.0).astype(bf16)
        select_ref[:, j * LANES : (j + 1) * LANES] = block
        slot_gate = slot_gate + jnp.where(here, spread_gate, 0.0)
    total = jnp.sum(slot_gate, axis=1, keepdims=True)
    gate_ref[...] = jnp.broadcast_to(total, (slots, LANES)).astype(bf16)


def route(z, pieces, column):
    whole = pl.BlockSpec((SLOTS, RING * LANES), lambda i: (0, 0))
    blocks = [
        pl.BlockSpec((LANES, LANES), lambda i, at=column if piece.shape[1] > LANES else 0: (0, at // LANES))
        for piece in pieces
    ]
    return pl.pallas_call(
        route_kernel,
        grid=(1,),
        out_shape=(
            jax.ShapeDtypeStruct((SLOTS, RING * LANES), bf16),
            jax.ShapeDtypeStruct((SLOTS, LANES), bf16),
        ),
        in_specs=[pl.BlockSpec(memory_space=pltpu.SMEM)] + blocks,
        out_specs=(whole, pl.BlockSpec((SLOTS, LANES), lambda i: (0, 0))),
        compiler_params=pltpu.CompilerParams(vmem_limit_bytes=VMEM_LIMIT),
        cost_estimate=pl.CostEstimate(flops=10**8, bytes_accessed=2 * 10**6, transcendentals=0),
        name="route",
    )(z, *pieces)


def pack_kernel(halfway, select_ref, gate_ref, *refs):
    pieces, (first_ref, second_ref), out_ref = refs[: RING - 1], refs[RING - 1 : RING + 1], refs[-1]
    middle = RING // 2
    step = pl.program_id(0)

    @pl.when(step < 2 * halfway)
    def _():
        far = jnp.where(step < halfway, first_ref[...], second_ref[...])
        rows = [piece[...] for piece in pieces]
        rows = jnp.concatenate(rows[:middle] + [far] + rows[middle:], axis=0)
        out_ref[...] = jnp.dot(select_ref[...], rows, preferred_element_type=f32).astype(bf16)

    @pl.when(step == 2 * halfway)
    def _():
        out_ref[:, :LANES] = gate_ref[...]


def pack(select, gate_column, pieces, first, second):
    tile = 384
    halfway = RING_SPLIT // tile
    width = 2 * RING_SPLIT
    near = pl.BlockSpec((LANES, tile), lambda i: (0, jnp.minimum(i, 2 * halfway - 1)))
    middle = RING // 2
    return pl.pallas_call(
        functools.partial(pack_kernel, halfway),
        grid=(2 * halfway + 1,),
        out_shape=pltpu.HBM((SLOTS, width + LANES), bf16),
        in_specs=[
            pl.BlockSpec((SLOTS, RING * LANES), lambda i: (0, 0)),
            pl.BlockSpec((SLOTS, LANES), lambda i: (0, 0)),
        ]
        + [near] * (RING - 1)
        + [
            pl.BlockSpec((LANES, tile), lambda i: (0, jnp.minimum(i, halfway - 1))),
            pl.BlockSpec((LANES, tile), lambda i: (0, jnp.clip(i - halfway, 0, halfway - 1))),
        ],
        out_specs=pl.BlockSpec((SLOTS, tile), lambda i: (0, i)),
        compiler_params=pltpu.CompilerParams(vmem_limit_bytes=VMEM_LIMIT),
        cost_estimate=pl.CostEstimate(
            flops=2 * SLOTS * RING * LANES * width,
            bytes_accessed=2 * width * (SLOTS + RING * LANES) + 2 * SLOTS * RING * LANES,
            transcendentals=0,
        ),
        name="pack",
    )(select, gate_column, *pieces[:middle], *pieces[middle + 1 :], first, second)


def ranks(code):
    expert = lax.broadcasted_iota(jnp.int32, (LANES, LANES), 0).astype(f32)
    match = jnp.zeros((LANES, LANES), f32)
    for k in range(TOPK):
        match = match + jnp.where(expert == code[k : k + 1], 1.0, 0.0)
    before = (
        lax.broadcasted_iota(jnp.int32, (LANES, LANES), 0)
        < lax.broadcasted_iota(jnp.int32, (LANES, LANES), 1)
    ).astype(bf16)
    return expert, match, jnp.dot(match.astype(bf16), before, preferred_element_type=f32)


def choose(code):
    unused, match, rank = ranks(code)
    order = (match * (rank + 1.0)).astype(bf16)
    row = lax.broadcasted_iota(jnp.int32, (SLOTS, LANES), 0)
    spread = (row // CAP == lax.broadcasted_iota(jnp.int32, (SLOTS, LANES), 1)).astype(bf16)
    order = jnp.dot(spread, order, preferred_element_type=f32)
    return order == (row % CAP + 1).astype(f32)


def own_kernel(info_ref, x_ref, *refs):
    out_ref, chosen_ref = refs[-2:]

    @pl.when(pl.program_id(0) == 0)
    def _():
        chosen = choose(info_ref[...].astype(f32).T[:TOPK])
        chosen_ref[...] = jnp.where(chosen, 1.0, 0.0).astype(bf16)

    out_ref[...] = jnp.dot(chosen_ref[...], x_ref[...], preferred_element_type=f32).astype(bf16)


def own_slots(info, x, later):
    width = x.shape[1]
    tile = 256
    return pl.pallas_call(
        own_kernel,
        grid=(width // tile,),
        out_shape=jax.ShapeDtypeStruct((SLOTS, width), bf16),
        in_specs=[
            pl.BlockSpec((LANES, LANES), lambda i: (0, 0)),
            pl.BlockSpec((LANES, tile), lambda i: (0, i)),
        ]
        + [pl.BlockSpec(memory_space=pl.ANY)] * len(later),
        out_specs=pl.BlockSpec((SLOTS, tile), lambda i: (0, i)),
        scratch_shapes=[pltpu.VMEM((SLOTS, LANES), bf16)],
        compiler_params=pltpu.CompilerParams(vmem_limit_bytes=VMEM_LIMIT),
        cost_estimate=pl.CostEstimate(
            flops=2 * SLOTS * LANES * width, bytes_accessed=2 * SLOTS * width, transcendentals=0
        ),
        name="own_slots",
    )(info, x, *later)


def moved_rows(z, turned):
    place = lax.broadcasted_iota(jnp.int32, (SLOTS, SLOTS), 0 if turned else 1)
    moved = lax.broadcasted_iota(jnp.int32, (SLOTS, SLOTS), 1 if turned else 0)
    step, rest = moved // (NODES * CAP), moved % (NODES * CAP)
    at = lax.rem(z + (RING - step if turned else step), RING)
    return jnp.where(place == rest // CAP * BLOCK + at * CAP + rest % CAP, 1.0, 0.0).astype(bf16)


def turn_kernel(z_ref, x_ref, *refs):
    outs, move_ref = refs[:-1], refs[-1]

    @pl.when(pl.program_id(0) == 0)
    def _():
        move_ref[...] = moved_rows(z_ref[0], False)

    rows = jnp.dot(move_ref[...], x_ref[...], preferred_element_type=f32).astype(bf16)
    part, middle = NODES * CAP, RING // 2
    blocks = [rows[k * part : (k + 1) * part] for k in range(RING)]
    blocks[2] = jnp.concatenate([blocks[2], blocks[middle][: part // 2]], axis=0)
    blocks[-2] = jnp.concatenate([blocks[-2], blocks[middle][part // 2 :]], axis=0)
    for out, block in zip(outs, blocks[:middle] + blocks[middle + 1 :]):
        out[...] = block


def turn(z, x):
    width = x.shape[1]
    tile = 256
    part = NODES * CAP
    heights = [part, part, part + part // 2, part, part, part + part // 2, part]
    return pl.pallas_call(
        turn_kernel,
        grid=(width // tile,),
        out_shape=[jax.ShapeDtypeStruct((height, width), bf16) for height in heights],
        in_specs=[
            pl.BlockSpec(memory_space=pltpu.SMEM),
            pl.BlockSpec((SLOTS, tile), lambda i: (0, i)),
        ],
        out_specs=[pl.BlockSpec((height, tile), lambda i: (0, i)) for height in heights],
        scratch_shapes=[pltpu.VMEM((SLOTS, SLOTS), bf16)],
        compiler_params=pltpu.CompilerParams(vmem_limit_bytes=VMEM_LIMIT),
        cost_estimate=pl.CostEstimate(
            flops=2 * SLOTS * SLOTS * width, bytes_accessed=4 * SLOTS * width, transcendentals=0
        ),
        name="turn",
    )(z, x)


def cross(blocks):
    def step(x, k):
        return lax.ppermute(x, "local", [(i, (i + k) % RING) for i in range(RING)])

    part = NODES * CAP
    zero, one, two, three, back3, back2, back1 = blocks
    two, back2 = step(two, 2), step(back2, -2)
    ahead, behind = step(two[part:], 2), step(back2[part:], -2)
    return [zero, step(one, 1), two, step(three, 3), ahead, behind, step(back3, -3), back2, step(back1, -1)]


def settle_kernel(z_ref, *refs):
    pieces, out_ref, move_ref = refs[:-2], refs[-2], refs[-1]

    @pl.when(pl.program_id(0) == 0)
    def _():
        move_ref[...] = moved_rows(z_ref[0], True)

    rows = jnp.concatenate([piece[...] for piece in pieces], axis=0)
    out_ref[...] = jnp.dot(move_ref[...], rows, preferred_element_type=f32).astype(bf16)


def settle(z, pieces):
    width = pieces[0].shape[1]
    tile = 256
    return pl.pallas_call(
        settle_kernel,
        grid=(width // tile,),
        out_shape=jax.ShapeDtypeStruct((SLOTS, width), bf16),
        in_specs=[pl.BlockSpec(memory_space=pltpu.SMEM)]
        + [
            pl.BlockSpec((min(piece.shape[0], NODES * CAP), tile), lambda i: (0, i))
            for piece in pieces
        ],
        out_specs=pl.BlockSpec((SLOTS, tile), lambda i: (0, i)),
        scratch_shapes=[pltpu.VMEM((SLOTS, SLOTS), bf16)],
        compiler_params=pltpu.CompilerParams(vmem_limit_bytes=VMEM_LIMIT),
        cost_estimate=pl.CostEstimate(
            flops=2 * SLOTS * SLOTS * width, bytes_accessed=4 * SLOTS * width, transcendentals=0
        ),
        name="settle",
    )(z, *pieces)


def halves_kernel(up_ref, down_ref, *refs):
    refs[-2][...] = up_ref[...]
    refs[-1][...] = down_ref[...]


def halves(up, down, later):
    tile = 384
    steps = RING_SPLIT // tile
    line = lambda i: (0, i)
    return pl.pallas_call(
        halves_kernel,
        grid=(steps,),
        out_shape=(jax.ShapeDtypeStruct((LANES, RING_SPLIT), bf16),) * 2,
        in_specs=[
            pl.BlockSpec((LANES, tile), line),
            pl.BlockSpec((LANES, tile), lambda i: (0, i + steps)),
        ]
        + [pl.BlockSpec(memory_space=pl.ANY)] * len(later),
        out_specs=(pl.BlockSpec((LANES, tile), line),) * 2,
        compiler_params=pltpu.CompilerParams(vmem_limit_bytes=VMEM_LIMIT),
        cost_estimate=pl.CostEstimate(flops=0, bytes_accessed=10**6, transcendentals=0),
        name="halves",
    )(up, down, *later)


def ring(block):
    ahead = [(i, (i + 1) % RING) for i in range(RING)]
    back = [(i, (i - 1) % RING) for i in range(RING)]
    pieces = [block] + [None] * (RING - 1)
    up = down = block
    for step in range(1, RING // 2):
        up = lax.ppermute(up, "local", ahead)
        down = lax.ppermute(down, "local", back)
        pieces[step], pieces[RING - step] = up, down
    return pieces


def farthest(up, down, later):
    ahead = [(i, (i + 1) % RING) for i in range(RING)]
    back = [(i, (i - 1) % RING) for i in range(RING)]
    first, second = halves(up, down, later)
    return lax.ppermute(first, "local", ahead), lax.ppermute(second, "local", back)


def back_kernel(rest, rows_ref, early_ref, hidden_ref, other_ref, own_ref, grad_ref, sums_ref, gated_ref):
    half = other_ref.shape[0]
    wide = half + rest
    total = jnp.dot(rows_ref[:, :half], other_ref[...], preferred_element_type=f32)
    total = total + jnp.dot(rows_ref[:, half:wide], own_ref[:rest], preferred_element_type=f32)
    total = total + jnp.dot(early_ref[...], own_ref[rest:], preferred_element_type=f32)
    gate = rows_ref[:, wide : wide + 1].astype(f32)
    hidden = hidden_ref[...].astype(f32)
    grad_ref[...] = (gate * total).astype(bf16)
    gated_ref[...] = (gate * hidden).astype(bf16)
    tile = rows_ref.shape[0]
    sums = jnp.sum(hidden * total, axis=1, keepdims=True)
    lane = lax.broadcasted_iota(jnp.int32, (tile, LANES), 1)
    rank = lax.broadcasted_iota(jnp.int32, (tile, LANES), 0) % CAP
    expert = lax.broadcasted_iota(jnp.int32, (tile // CAP, tile), 0)
    gather = jnp.where(expert == lax.broadcasted_iota(jnp.int32, expert.shape, 1) // CAP, 1.0, 0.0)
    sums_ref[...] = jnp.dot(
        gather,
        jnp.where(lane == rank, sums, 0.0),
        precision=lax.Precision.HIGHEST,
        preferred_element_type=f32,
    )


def back(rows, early, hidden, weight_other, weight_own):
    tile = 384
    half, units = weight_other.shape
    line = lambda i: (i, 0)
    still = pl.BlockSpec((half, units), lambda i: (0, 0), pipeline_mode=pl.Buffered(1))
    return pl.pallas_call(
        functools.partial(back_kernel, half - early.shape[1]),
        grid=(SLOTS // tile,),
        out_shape=(
            jax.ShapeDtypeStruct((SLOTS, units), bf16),
            jax.ShapeDtypeStruct((SLOTS // CAP, LANES), f32),
            jax.ShapeDtypeStruct((SLOTS, units), bf16),
        ),
        in_specs=[
            pl.BlockSpec((tile, rows.shape[1]), line),
            pl.BlockSpec((tile, early.shape[1]), line),
            pl.BlockSpec((tile, units), line),
            still,
            still,
        ],
        out_specs=(
            pl.BlockSpec((tile, units), line),
            pl.BlockSpec((tile // CAP, LANES), line),
            pl.BlockSpec((tile, units), line),
        ),
        compiler_params=pltpu.CompilerParams(vmem_limit_bytes=32 * 2**20),
        cost_estimate=pl.CostEstimate(
            flops=4 * SLOTS * units * half, bytes_accessed=18 * 10**6, transcendentals=0
        ),
        name="back",
    )(rows, early, hidden, weight_other, weight_own)


def down_kernel(steps, x_ref, y_ref, gated_ref, received_ref, out_ref, mark_ref):
    mark_ref[...] = jnp.zeros_like(mark_ref)
    step = pl.program_id(0)
    rows = jnp.where(step < steps, x_ref[...], y_ref[...])
    share = lax.dot_general(rows, gated_ref[...], (((0,), (0,)), ((), ())), preferred_element_type=f32)
    out_ref[...] = (share + received_ref[...].astype(f32)).astype(bf16)


def down(x, skip, y, gated, received):
    tile = 256
    more = y.shape[1] // tile
    steps = received.shape[0] // tile - more
    units = gated.shape[1]
    return pl.pallas_call(
        functools.partial(down_kernel, steps),
        grid=(steps + more,),
        out_shape=(
            jax.ShapeDtypeStruct(received.shape, bf16),
            jax.ShapeDtypeStruct((8, LANES), f32),
        ),
        in_specs=[
            pl.BlockSpec((SLOTS, tile), lambda i: (0, skip // tile + jnp.minimum(i, steps - 1))),
            pl.BlockSpec((SLOTS, tile), lambda i: (0, jnp.maximum(i - steps, 0))),
            pl.BlockSpec((SLOTS, units), lambda i: (0, 0)),
            pl.BlockSpec((tile, units), lambda i: (i, 0)),
        ],
        out_specs=(
            pl.BlockSpec((tile, units), lambda i: (i, 0)),
            pl.BlockSpec((8, LANES), lambda i: (0, 0)),
        ),
        compiler_params=pltpu.CompilerParams(vmem_limit_bytes=VMEM_LIMIT),
        cost_estimate=pl.CostEstimate(
            flops=2 * SLOTS * units * received.shape[0], bytes_accessed=12 * 10**6, transcendentals=0
        ),
        name="down",
    )(x, y, gated, received)


def finish_kernel(info_ref, logits_ref, value_ref, *refs):
    out_ref = refs[-1]
    code = info_ref[...].astype(f32).T[:TOPK]
    expert, match, rank = ranks(code)
    value = jnp.zeros((LANES, LANES), f32)
    for c in range(CAP):
        value = jnp.where(rank == float(c), value_ref[:, c : c + 1], value)
    value = jnp.where(match > 0.0, value, 0.0)
    pairs = [
        jnp.sum(jnp.where(expert == code[k : k + 1], value, 0.0), axis=0, keepdims=True)
        for k in range(TOPK)
    ]
    pair_grad = jnp.concatenate(pairs, axis=0)
    affinity = 1.0 / (1.0 + jnp.exp(-logits_ref[...]))
    denominator = jnp.sum(affinity, axis=0, keepdims=True)
    weighted = jnp.sum(pair_grad * affinity, axis=0, keepdims=True)
    grad = route_scale * (pair_grad / denominator - weighted / (denominator * denominator))
    out_ref[...] = grad * affinity * (1.0 - affinity)


def finish(info, logits, value, later):
    vmem = pl.BlockSpec(memory_space=pltpu.VMEM)
    return pl.pallas_call(
        finish_kernel,
        out_shape=jax.ShapeDtypeStruct(logits.shape, f32),
        in_specs=[vmem] * 3 + [pl.BlockSpec(memory_space=pl.ANY)] * len(later),
        out_specs=vmem,
        compiler_params=pltpu.CompilerParams(vmem_limit_bytes=VMEM_LIMIT),
        cost_estimate=pl.CostEstimate(flops=10**7, bytes_accessed=10**6, transcendentals=10**4),
        name="finish",
    )(info, logits, value, *later)


def local(out_grad, expert_ids, drop_flags, router_logits, saved_hidden, down_weight):
    slot_total = saved_hidden.shape[2]
    half = out_grad.shape[1] // 2
    experts = NODES * RING
    z = lax.axis_index("local")
    copy = lax.axis_index("replica")
    swap = [(0, 1), (1, 0)]

    info = codes(expert_ids, drop_flags, router_logits)

    weight_own = down_weight.reshape(half, down_weight.shape[2])
    weight_other = lax.ppermute(weight_own, "replica", swap)
    hidden = saved_hidden.reshape(slot_total, saved_hidden.shape[3])

    low, high = out_grad[:, :half], out_grad[:, half:]
    other, own = jnp.where(copy == 0, high, low), jnp.where(copy == 0, low, high)
    at = z.reshape(1)
    rest = half - EARLY
    wide = half + rest

    middle = RING // 2
    pieces = ring(jnp.concatenate([other, own[:, :rest], info], axis=1))
    far_info = lax.ppermute(info, "local", [(i, (i + middle) % RING) for i in range(RING)])

    early = own_slots(info, own[:, rest:], ())
    early = early.reshape(NODES, BLOCK, EARLY)
    early = lax.all_to_all(early, "node", split_axis=0, concat_axis=0, tiled=True)
    early = turn(at, early.reshape(slot_total, EARLY))
    first, second = farthest(pieces[middle - 1], pieces[middle + 1], (far_info,))
    crossed = cross(early)
    select, gate_column = route(at, pieces[:middle] + [far_info] + pieces[middle + 1 :], wide)
    rows = pack(select, gate_column, pieces, first, second)
    rows = rows.reshape(NODES, BLOCK, wide + LANES)
    rows = lax.all_to_all(rows, "node", split_axis=0, concat_axis=0, tiled=True)
    rows = rows.reshape(slot_total, wide + LANES)

    early = settle(at, crossed)
    grad_hidden, gate_grad, gated = back(rows, early, hidden, weight_other, weight_own)
    grad_hidden = grad_hidden.reshape(saved_hidden.shape)
    returned = lax.all_to_all(
        gate_grad[:, :CAP],
        ("node", "local"),
        split_axis=0,
        concat_axis=0,
        tiled=True,
    )
    received = lax.dot_general(
        rows[:, :half], gated, (((0,), (0,)), ((), ())), preferred_element_type=f32
    )
    received = lax.ppermute(received.astype(bf16), "replica", swap)
    grad_down, mark = down(rows, half, early, gated, received)
    grad_logits = finish(info, router_logits.T, returned, (mark,)).T
    return (grad_logits, grad_hidden, grad_down.reshape(down_weight.shape))


def solution(mesh):
    return jax.shard_map(
        local,
        mesh=mesh,
        in_specs=(
            P(("node", "local", "replica"), None),
            P(("node", "local", "replica"), None),
            P(("node", "local", "replica"), None),
            P(("node", "local", "replica"), None),
            P("replica", ("node", "local"), None, None),
            P(("node", "local"), "replica", None),
        ),
        out_specs=(
            P(("node", "local", "replica"), None),
            P("replica", ("node", "local"), None, None),
            P(("node", "local"), "replica", None),
        ),
        check_vma=False,
    )
```

```python
import functools

import jax
import jax.numpy as jnp
from jax import lax
from jax.experimental import pallas as pl
from jax.experimental.pallas import tpu as pltpu
from jax.sharding import PartitionSpec as P

route_scale = 2.5
bf16 = jnp.bfloat16
f32 = jnp.float32
EARLY = 1024
NODES = 16
RING = 8
CAP = 6
TOPK = 8
BLOCK = RING * CAP
LANES = 128
SLOTS = NODES * BLOCK
RING_SPLIT = 1280
VMEM_LIMIT = 14 * 2**20


def codes_kernel(ids_ref, drop_ref, logits_ref, out_ref):
    code = jnp.where(drop_ref[...] == 0, ids_ref[...], -1).astype(f32)
    affinity = 1.0 / (1.0 + jnp.exp(-logits_ref[...]))
    gate = route_scale * affinity / jnp.sum(affinity, axis=0, keepdims=True)
    rest = jnp.zeros((LANES - 2 * TOPK, LANES), f32)
    out_ref[...] = jnp.concatenate([code, gate, rest], axis=0).T.astype(bf16)


def codes(expert_ids, drop_flags, router_logits):
    vmem = pl.BlockSpec(memory_space=pltpu.VMEM)
    return pl.pallas_call(
        codes_kernel,
        out_shape=jax.ShapeDtypeStruct((LANES, LANES), bf16),
        in_specs=[vmem] * 3,
        out_specs=vmem,
        compiler_params=pltpu.CompilerParams(vmem_limit_bytes=VMEM_LIMIT),
        cost_estimate=pl.CostEstimate(flops=10**5, bytes_accessed=10**5, transcendentals=10**3),
        name="codes",
    )(expert_ids.T, drop_flags.T, router_logits.T)


def route_kernel(z_ref, *refs):
    infos, (select_ref, gate_ref) = refs[:RING], refs[RING:]
    slots = SLOTS
    z = z_ref[0]
    expert = (lax.broadcasted_iota(jnp.int32, (NODES, LANES), 0) * RING + z).astype(f32)
    before = (
        lax.broadcasted_iota(jnp.int32, (LANES, LANES), 0)
        < lax.broadcasted_iota(jnp.int32, (LANES, LANES), 1)
    ).astype(bf16)
    spread = (
        lax.broadcasted_iota(jnp.int32, (slots, NODES), 0) // BLOCK
        == lax.broadcasted_iota(jnp.int32, (slots, NODES), 1)
    ).astype(bf16)
    row = lax.broadcasted_iota(jnp.int32, (slots, LANES), 0) % BLOCK
    source = row // CAP
    wanted = (row % CAP + 1).astype(f32)
    slot_gate = jnp.zeros((slots, LANES), f32)
    for j in range(RING):
        info = infos[j][...].astype(f32).T
        code, gate = info[:TOPK], info[TOPK : 2 * TOPK]
        match = jnp.zeros((NODES, LANES), f32)
        match_gate = jnp.zeros((NODES, LANES), f32)
        for k in range(TOPK):
            hit = expert == code[k : k + 1]
            match = match + jnp.where(hit, 1.0, 0.0)
            match_gate = match_gate + jnp.where(hit, gate[k : k + 1], 0.0)
        rank = jnp.dot(match.astype(bf16), before, preferred_element_type=f32)
        order = (match * (rank + 1.0)).astype(bf16)
        order = jnp.dot(spread, order, preferred_element_type=f32)
        spread_gate = jnp.dot(spread, match_gate.astype(bf16), preferred_element_type=f32)
        origin = lax.rem(z + RING - j, RING)
        here = (order == wanted) & (source == origin)
        block = jnp.where(here, 1.0, 0.0).astype(bf16)
        select_ref[:, j * LANES : (j + 1) * LANES] = block
        slot_gate = slot_gate + jnp.where(here, spread_gate, 0.0)
    total = jnp.sum(slot_gate, axis=1, keepdims=True)
    gate_ref[...] = jnp.broadcast_to(total, (slots, LANES)).astype(bf16)


def route(z, pieces, column):
    whole = pl.BlockSpec((SLOTS, RING * LANES), lambda i: (0, 0))
    blocks = [
        pl.BlockSpec((LANES, LANES), lambda i, at=column if piece.shape[1] > LANES else 0: (0, at // LANES))
        for piece in pieces
    ]
    return pl.pallas_call(
        route_kernel,
        grid=(1,),
        out_shape=(
            jax.ShapeDtypeStruct((SLOTS, RING * LANES), bf16),
            jax.ShapeDtypeStruct((SLOTS, LANES), bf16),
        ),
        in_specs=[pl.BlockSpec(memory_space=pltpu.SMEM)] + blocks,
        out_specs=(whole, pl.BlockSpec((SLOTS, LANES), lambda i: (0, 0))),
        compiler_params=pltpu.CompilerParams(vmem_limit_bytes=VMEM_LIMIT),
        cost_estimate=pl.CostEstimate(flops=10**8, bytes_accessed=2 * 10**6, transcendentals=0),
        name="route",
    )(z, *pieces)


def pack_kernel(halfway, select_ref, gate_ref, *refs):
    pieces, (first_ref, second_ref), out_ref = refs[: RING - 1], refs[RING - 1 : RING + 1], refs[-1]
    middle = RING // 2
    step = pl.program_id(0)

    @pl.when(step < 2 * halfway)
    def _():
        far = jnp.where(step < halfway, first_ref[...], second_ref[...])
        rows = [piece[...] for piece in pieces]
        rows = jnp.concatenate(rows[:middle] + [far] + rows[middle:], axis=0)
        out_ref[...] = jnp.dot(select_ref[...], rows, preferred_element_type=f32).astype(bf16)

    @pl.when(step == 2 * halfway)
    def _():
        out_ref[:, :LANES] = gate_ref[...]


def pack(select, gate_column, pieces, first, second):
    tile = 640
    halfway = RING_SPLIT // tile
    width = 2 * RING_SPLIT
    near = pl.BlockSpec((LANES, tile), lambda i: (0, jnp.minimum(i, 2 * halfway - 1)))
    middle = RING // 2
    return pl.pallas_call(
        functools.partial(pack_kernel, halfway),
        grid=(2 * halfway + 1,),
        out_shape=pltpu.HBM((SLOTS, width + LANES), bf16),
        in_specs=[
            pl.BlockSpec((SLOTS, RING * LANES), lambda i: (0, 0)),
            pl.BlockSpec((SLOTS, LANES), lambda i: (0, 0)),
        ]
        + [near] * (RING - 1)
        + [
            pl.BlockSpec((LANES, tile), lambda i: (0, jnp.minimum(i, halfway - 1))),
            pl.BlockSpec((LANES, tile), lambda i: (0, jnp.clip(i - halfway, 0, halfway - 1))),
        ],
        out_specs=pl.BlockSpec((SLOTS, tile), lambda i: (0, i)),
        compiler_params=pltpu.CompilerParams(vmem_limit_bytes=VMEM_LIMIT),
        cost_estimate=pl.CostEstimate(
            flops=2 * SLOTS * RING * LANES * width,
            bytes_accessed=2 * width * (SLOTS + RING * LANES) + 2 * SLOTS * RING * LANES,
            transcendentals=0,
        ),
        name="pack",
    )(select, gate_column, *pieces[:middle], *pieces[middle + 1 :], first, second)


def ranks(code):
    expert = lax.broadcasted_iota(jnp.int32, (LANES, LANES), 0).astype(f32)
    match = jnp.zeros((LANES, LANES), f32)
    for k in range(TOPK):
        match = match + jnp.where(expert == code[k : k + 1], 1.0, 0.0)
    before = (
        lax.broadcasted_iota(jnp.int32, (LANES, LANES), 0)
        < lax.broadcasted_iota(jnp.int32, (LANES, LANES), 1)
    ).astype(bf16)
    return expert, match, jnp.dot(match.astype(bf16), before, preferred_element_type=f32)


def choose(code):
    unused, match, rank = ranks(code)
    order = (match * (rank + 1.0)).astype(bf16)
    row = lax.broadcasted_iota(jnp.int32, (SLOTS, LANES), 0)
    spread = (row // CAP == lax.broadcasted_iota(jnp.int32, (SLOTS, LANES), 1)).astype(bf16)
    order = jnp.dot(spread, order, preferred_element_type=f32)
    return order == (row % CAP + 1).astype(f32)


def own_kernel(info_ref, x_ref, *refs):
    out_ref, chosen_ref = refs[-2:]

    @pl.when(pl.program_id(0) == 0)
    def _():
        chosen = choose(info_ref[...].astype(f32).T[:TOPK])
        chosen_ref[...] = jnp.where(chosen, 1.0, 0.0).astype(bf16)

    out_ref[...] = jnp.dot(chosen_ref[...], x_ref[...], preferred_element_type=f32).astype(bf16)


def own_slots(info, x, later):
    width = x.shape[1]
    tile = 256
    return pl.pallas_call(
        own_kernel,
        grid=(width // tile,),
        out_shape=jax.ShapeDtypeStruct((SLOTS, width), bf16),
        in_specs=[
            pl.BlockSpec((LANES, LANES), lambda i: (0, 0)),
            pl.BlockSpec((LANES, tile), lambda i: (0, i)),
        ]
        + [pl.BlockSpec(memory_space=pl.ANY)] * len(later),
        out_specs=pl.BlockSpec((SLOTS, tile), lambda i: (0, i)),
        scratch_shapes=[pltpu.VMEM((SLOTS, LANES), bf16)],
        compiler_params=pltpu.CompilerParams(vmem_limit_bytes=VMEM_LIMIT),
        cost_estimate=pl.CostEstimate(
            flops=2 * SLOTS * LANES * width, bytes_accessed=2 * SLOTS * width, transcendentals=0
        ),
        name="own_slots",
    )(info, x, *later)


def moved_rows(z, turned):
    place = lax.broadcasted_iota(jnp.int32, (SLOTS, SLOTS), 0 if turned else 1)
    moved = lax.broadcasted_iota(jnp.int32, (SLOTS, SLOTS), 1 if turned else 0)
    step, rest = moved // (NODES * CAP), moved % (NODES * CAP)
    at = lax.rem(z + (RING - step if turned else step), RING)
    return jnp.where(place == rest // CAP * BLOCK + at * CAP + rest % CAP, 1.0, 0.0).astype(bf16)


def turn_kernel(z_ref, x_ref, *refs):
    outs, move_ref = refs[:-1], refs[-1]

    @pl.when(pl.program_id(0) == 0)
    def _():
        move_ref[...] = moved_rows(z_ref[0], False)

    rows = jnp.dot(move_ref[...], x_ref[...], preferred_element_type=f32).astype(bf16)
    part, middle = NODES * CAP, RING // 2
    blocks = [rows[k * part : (k + 1) * part] for k in range(RING)]
    blocks[2] = jnp.concatenate([blocks[2], blocks[middle][: part // 2]], axis=0)
    blocks[-2] = jnp.concatenate([blocks[-2], blocks[middle][part // 2 :]], axis=0)
    for out, block in zip(outs, blocks[:middle] + blocks[middle + 1 :]):
        out[...] = block


def turn(z, x):
    width = x.shape[1]
    tile = 256
    part = NODES * CAP
    heights = [part, part, part + part // 2, part, part, part + part // 2, part]
    return pl.pallas_call(
        turn_kernel,
        grid=(width // tile,),
        out_shape=[jax.ShapeDtypeStruct((height, width), bf16) for height in heights],
        in_specs=[
            pl.BlockSpec(memory_space=pltpu.SMEM),
            pl.BlockSpec((SLOTS, tile), lambda i: (0, i)),
        ],
        out_specs=[pl.BlockSpec((height, tile), lambda i: (0, i)) for height in heights],
        scratch_shapes=[pltpu.VMEM((SLOTS, SLOTS), bf16)],
        compiler_params=pltpu.CompilerParams(vmem_limit_bytes=VMEM_LIMIT),
        cost_estimate=pl.CostEstimate(
            flops=2 * SLOTS * SLOTS * width, bytes_accessed=4 * SLOTS * width, transcendentals=0
        ),
        name="turn",
    )(z, x)


def cross(blocks):
    def step(x, k):
        return lax.ppermute(x, "local", [(i, (i + k) % RING) for i in range(RING)])

    part = NODES * CAP
    zero, one, two, three, back3, back2, back1 = blocks
    two, back2 = step(two, 2), step(back2, -2)
    ahead, behind = step(two[part:], 2), step(back2[part:], -2)
    return [zero, step(one, 1), two, step(three, 3), ahead, behind, step(back3, -3), back2, step(back1, -1)]


def settle_kernel(z_ref, *refs):
    pieces, out_ref, move_ref = refs[:-2], refs[-2], refs[-1]

    @pl.when(pl.program_id(0) == 0)
    def _():
        move_ref[...] = moved_rows(z_ref[0], True)

    rows = jnp.concatenate([piece[...] for piece in pieces], axis=0)
    out_ref[...] = jnp.dot(move_ref[...], rows, preferred_element_type=f32).astype(bf16)


def settle(z, pieces):
    width = pieces[0].shape[1]
    tile = 256
    return pl.pallas_call(
        settle_kernel,
        grid=(width // tile,),
        out_shape=jax.ShapeDtypeStruct((SLOTS, width), bf16),
        in_specs=[pl.BlockSpec(memory_space=pltpu.SMEM)]
        + [
            pl.BlockSpec((min(piece.shape[0], NODES * CAP), tile), lambda i: (0, i))
            for piece in pieces
        ],
        out_specs=pl.BlockSpec((SLOTS, tile), lambda i: (0, i)),
        scratch_shapes=[pltpu.VMEM((SLOTS, SLOTS), bf16)],
        compiler_params=pltpu.CompilerParams(vmem_limit_bytes=VMEM_LIMIT),
        cost_estimate=pl.CostEstimate(
            flops=2 * SLOTS * SLOTS * width, bytes_accessed=4 * SLOTS * width, transcendentals=0
        ),
        name="settle",
    )(z, *pieces)


def halves_kernel(up_ref, down_ref, *refs):
    refs[-2][...] = up_ref[...]
    refs[-1][...] = down_ref[...]


def halves(up, down, later):
    tile = 256
    steps = RING_SPLIT // tile
    line = lambda i: (0, i)
    return pl.pallas_call(
        halves_kernel,
        grid=(steps,),
        out_shape=(jax.ShapeDtypeStruct((LANES, RING_SPLIT), bf16),) * 2,
        in_specs=[
            pl.BlockSpec((LANES, tile), line),
            pl.BlockSpec((LANES, tile), lambda i: (0, i + steps)),
        ]
        + [pl.BlockSpec(memory_space=pl.ANY)] * len(later),
        out_specs=(pl.BlockSpec((LANES, tile), line),) * 2,
        compiler_params=pltpu.CompilerParams(vmem_limit_bytes=VMEM_LIMIT),
        cost_estimate=pl.CostEstimate(flops=0, bytes_accessed=10**6, transcendentals=0),
        name="halves",
    )(up, down, *later)


def ring(block):
    ahead = [(i, (i + 1) % RING) for i in range(RING)]
    back = [(i, (i - 1) % RING) for i in range(RING)]
    pieces = [block] + [None] * (RING - 1)
    up = down = block
    for step in range(1, RING // 2):
        up = lax.ppermute(up, "local", ahead)
        down = lax.ppermute(down, "local", back)
        pieces[step], pieces[RING - step] = up, down
    return pieces


def farthest(up, down, later):
    ahead = [(i, (i + 1) % RING) for i in range(RING)]
    back = [(i, (i - 1) % RING) for i in range(RING)]
    first, second = halves(up, down, later)
    return lax.ppermute(first, "local", ahead), lax.ppermute(second, "local", back)


def back_kernel(rest, rows_ref, early_ref, hidden_ref, other_ref, own_ref, grad_ref, sums_ref, gated_ref):
    half = other_ref.shape[0]
    wide = half + rest
    total = jnp.dot(rows_ref[:, :half], other_ref[...], preferred_element_type=f32)
    total = total + jnp.dot(rows_ref[:, half:wide], own_ref[:rest], preferred_element_type=f32)
    total = total + jnp.dot(early_ref[...], own_ref[rest:], preferred_element_type=f32)
    gate = rows_ref[:, wide : wide + 1].astype(f32)
    hidden = hidden_ref[...].astype(f32)
    grad_ref[...] = (gate * total).astype(bf16)
    gated_ref[...] = (gate * hidden).astype(bf16)
    tile = rows_ref.shape[0]
    sums = jnp.sum(hidden * total, axis=1, keepdims=True)
    lane = lax.broadcasted_iota(jnp.int32, (tile, LANES), 1)
    rank = lax.broadcasted_iota(jnp.int32, (tile, LANES), 0) % CAP
    expert = lax.broadcasted_iota(jnp.int32, (tile // CAP, tile), 0)
    gather = jnp.where(expert == lax.broadcasted_iota(jnp.int32, expert.shape, 1) // CAP, 1.0, 0.0)
    sums_ref[...] = jnp.dot(
        gather,
        jnp.where(lane == rank, sums, 0.0),
        precision=lax.Precision.HIGHEST,
        preferred_element_type=f32,
    )


def back(rows, early, hidden, weight_other, weight_own):
    tile = 384
    half, units = weight_other.shape
    line = lambda i: (i, 0)
    still = pl.BlockSpec((half, units), lambda i: (0, 0), pipeline_mode=pl.Buffered(1))
    return pl.pallas_call(
        functools.partial(back_kernel, half - early.shape[1]),
        grid=(SLOTS // tile,),
        out_shape=(
            jax.ShapeDtypeStruct((SLOTS, units), bf16),
            jax.ShapeDtypeStruct((SLOTS // CAP, LANES), f32),
            jax.ShapeDtypeStruct((SLOTS, units), bf16),
        ),
        in_specs=[
            pl.BlockSpec((tile, rows.shape[1]), line),
            pl.BlockSpec((tile, early.shape[1]), line),
            pl.BlockSpec((tile, units), line),
            still,
            still,
        ],
        out_specs=(
            pl.BlockSpec((tile, units), line),
            pl.BlockSpec((tile // CAP, LANES), line),
            pl.BlockSpec((tile, units), line),
        ),
        compiler_params=pltpu.CompilerParams(vmem_limit_bytes=32 * 2**20),
        cost_estimate=pl.CostEstimate(
            flops=4 * SLOTS * units * half, bytes_accessed=18 * 10**6, transcendentals=0
        ),
        name="back",
    )(rows, early, hidden, weight_other, weight_own)


def down_kernel(steps, x_ref, y_ref, gated_ref, received_ref, out_ref, mark_ref):
    mark_ref[...] = jnp.zeros_like(mark_ref)
    step = pl.program_id(0)
    rows = jnp.where(step < steps, x_ref[...], y_ref[...])
    share = lax.dot_general(rows, gated_ref[...], (((0,), (0,)), ((), ())), preferred_element_type=f32)
    out_ref[...] = (share + received_ref[...].astype(f32)).astype(bf16)


def down(x, skip, y, gated, received):
    tile = 256
    more = y.shape[1] // tile
    steps = received.shape[0] // tile - more
    units = gated.shape[1]
    return pl.pallas_call(
        functools.partial(down_kernel, steps),
        grid=(steps + more,),
        out_shape=(
            jax.ShapeDtypeStruct(received.shape, bf16),
            jax.ShapeDtypeStruct((8, LANES), f32),
        ),
        in_specs=[
            pl.BlockSpec((SLOTS, tile), lambda i: (0, skip // tile + jnp.minimum(i, steps - 1))),
            pl.BlockSpec((SLOTS, tile), lambda i: (0, jnp.maximum(i - steps, 0))),
            pl.BlockSpec((SLOTS, units), lambda i: (0, 0)),
            pl.BlockSpec((tile, units), lambda i: (i, 0)),
        ],
        out_specs=(
            pl.BlockSpec((tile, units), lambda i: (i, 0)),
            pl.BlockSpec((8, LANES), lambda i: (0, 0)),
        ),
        compiler_params=pltpu.CompilerParams(vmem_limit_bytes=VMEM_LIMIT),
        cost_estimate=pl.CostEstimate(
            flops=2 * SLOTS * units * received.shape[0], bytes_accessed=12 * 10**6, transcendentals=0
        ),
        name="down",
    )(x, y, gated, received)


def finish_kernel(info_ref, logits_ref, value_ref, *refs):
    out_ref = refs[-1]
    code = info_ref[...].astype(f32).T[:TOPK]
    expert, match, rank = ranks(code)
    value = jnp.zeros((LANES, LANES), f32)
    for c in range(CAP):
        value = jnp.where(rank == float(c), value_ref[:, c : c + 1], value)
    value = jnp.where(match > 0.0, value, 0.0)
    pairs = [
        jnp.sum(jnp.where(expert == code[k : k + 1], value, 0.0), axis=0, keepdims=True)
        for k in range(TOPK)
    ]
    pair_grad = jnp.concatenate(pairs, axis=0)
    affinity = 1.0 / (1.0 + jnp.exp(-logits_ref[...]))
    denominator = jnp.sum(affinity, axis=0, keepdims=True)
    weighted = jnp.sum(pair_grad * affinity, axis=0, keepdims=True)
    grad = route_scale * (pair_grad / denominator - weighted / (denominator * denominator))
    out_ref[...] = grad * affinity * (1.0 - affinity)


def finish(info, logits, value, later):
    vmem = pl.BlockSpec(memory_space=pltpu.VMEM)
    return pl.pallas_call(
        finish_kernel,
        out_shape=jax.ShapeDtypeStruct(logits.shape, f32),
        in_specs=[vmem] * 3 + [pl.BlockSpec(memory_space=pl.ANY)] * len(later),
        out_specs=vmem,
        compiler_params=pltpu.CompilerParams(vmem_limit_bytes=VMEM_LIMIT),
        cost_estimate=pl.CostEstimate(flops=10**7, bytes_accessed=10**6, transcendentals=10**4),
        name="finish",
    )(info, logits, value, *later)


def local(out_grad, expert_ids, drop_flags, router_logits, saved_hidden, down_weight):
    slot_total = saved_hidden.shape[2]
    half = out_grad.shape[1] // 2
    experts = NODES * RING
    z = lax.axis_index("local")
    copy = lax.axis_index("replica")
    swap = [(0, 1), (1, 0)]

    info = codes(expert_ids, drop_flags, router_logits)

    weight_own = down_weight.reshape(half, down_weight.shape[2])
    weight_other = lax.ppermute(weight_own, "replica", swap)
    hidden = saved_hidden.reshape(slot_total, saved_hidden.shape[3])

    low, high = out_grad[:, :half], out_grad[:, half:]
    other, own = jnp.where(copy == 0, high, low), jnp.where(copy == 0, low, high)
    at = z.reshape(1)
    rest = half - EARLY
    wide = half + rest

    middle = RING // 2
    pieces = ring(jnp.concatenate([other, own[:, :rest], info], axis=1))
    far_info = lax.ppermute(info, "local", [(i, (i + middle) % RING) for i in range(RING)])

    early = own_slots(info, own[:, rest:], ())
    early = early.reshape(NODES, BLOCK, EARLY)
    early = lax.all_to_all(early, "node", split_axis=0, concat_axis=0, tiled=True)
    early = turn(at, early.reshape(slot_total, EARLY))
    first, second = farthest(pieces[middle - 1], pieces[middle + 1], (far_info,))
    crossed = cross(early)
    select, gate_column = route(at, pieces[:middle] + [far_info] + pieces[middle + 1 :], wide)
    rows = pack(select, gate_column, pieces, first, second)
    rows = rows.reshape(NODES, BLOCK, wide + LANES)
    rows = lax.all_to_all(rows, "node", split_axis=0, concat_axis=0, tiled=True)
    rows = rows.reshape(slot_total, wide + LANES)

    early = settle(at, crossed)
    grad_hidden, gate_grad, gated = back(rows, early, hidden, weight_other, weight_own)
    grad_hidden = grad_hidden.reshape(saved_hidden.shape)
    returned = lax.all_to_all(
        gate_grad[:, :CAP],
        ("node", "local"),
        split_axis=0,
        concat_axis=0,
        tiled=True,
    )
    received = lax.dot_general(
        rows[:, :half], gated, (((0,), (0,)), ((), ())), preferred_element_type=f32
    )
    received = lax.ppermute(received.astype(bf16), "replica", swap)
    grad_down, mark = down(rows, half, early, gated, received)
    grad_logits = finish(info, router_logits.T, returned, (mark,)).T
    return (grad_logits, grad_hidden, grad_down.reshape(down_weight.shape))


def solution(mesh):
    return jax.shard_map(
        local,
        mesh=mesh,
        in_specs=(
            P(("node", "local", "replica"), None),
            P(("node", "local", "replica"), None),
            P(("node", "local", "replica"), None),
            P(("node", "local", "replica"), None),
            P("replica", ("node", "local"), None, None),
            P(("node", "local"), "replica", None),
        ),
        out_specs=(
            P(("node", "local", "replica"), None),
            P("replica", ("node", "local"), None, None),
            P(("node", "local"), "replica", None),
        ),
        check_vma=False,
    )
```
